128 devices in a mesh: dp: 32 (over z, y, core), replica: 4 (over x).
Axes of the slice: x: 4, y: 4, z: 4, core: 2. Of those that a mesh axis runs over, the one named last changes fastest.
Arguments:
- gradients: bfloat16 [64, 1024, 1024], P(None, 'dp')
- stat_left: float32 [64, 1024, 1024], P('dp', 'replica'), may hold values from -6 to 6
- stat_right: float32 [64, 1024, 1024], P('dp', 'replica'), may hold values from -6 to 6
- inv_left: bfloat16 [32, 4, 2, 1024, 1024], P('dp', 'replica')
- inv_right: bfloat16 [32, 4, 2, 1024, 1024], P('dp', 'replica')
- owned_blocks: int32 [32, 4, 2], replicated, may hold values from 0 to 1, as said below
- owner_counts: int32 [32, 4], replicated, may hold values from 0 to 2, as said below
- block_matrix: int32 [64], replicated, may hold values from 0 to 4
Outputs:
- update: bfloat16 [64, 1024, 1024], P(None, 'dp')
- new_left: float32 [64, 1024, 1024], P('dp', 'replica')
- new_right: float32 [64, 1024, 1024], P('dp', 'replica')
The draws below stay inside these ranges and needn't reach their ends.
Inputs may be any that keep to these rules, and one draw needn't show every extreme that they name: `owned_blocks`: at each dp index the first owner_counts entries of a replica's list name, in rising order, the local blocks that replica owns; each of the 2 local blocks has exactly one owner; entries past the count name other local blocks. `owner_counts`: the counts of a dp index sum to 2; at dp index 0 one replica owns all 2 blocks.
All inputs are finite; a program needn't handle non-finite values.
Results may differ from the reference program's by a relative error of at most 0.0058.
Values may be sent and summed in bfloat16 or wider, within the bound.
No kernel may reach another device: no remote copies, remote signals or barrier semaphores. Data moves between devices by JAX's collectives and lax.ppermute only.
A program may use at most 128 MiB of HBM per device.

```python
import jax
import jax.numpy as jnp
from jax import lax

B = 1024
BLK_DP = 2
NMAT = 5
SLOTS = 2
NBLK = 64
N_DP = 32
N_REPLICA = 4


def ownership(key):
    first_owner = jax.random.randint(jax.random.fold_in(key, 11), (1, 1), 0, N_REPLICA)
    other_owners = jax.random.randint(jax.random.fold_in(key, 12), (N_DP, BLK_DP), 0, N_REPLICA)
    dp_ids = jnp.arange(N_DP, dtype=jnp.int32)[:, None]
    owners = jnp.where(dp_ids == 0, first_owner, other_owners)
    replicas = jnp.arange(N_REPLICA, dtype=jnp.int32)
    belongs = owners[:, None, :] == replicas[None, :, None]
    local_ids = jnp.arange(BLK_DP, dtype=jnp.int32)
    scores = jnp.where(belongs, local_ids[None, None, :], local_ids[None, None, :] + BLK_DP)
    table = jnp.argsort(scores, axis=-1).astype(jnp.int32)
    number = jnp.sum(belongs.astype(jnp.int32), axis=-1).astype(jnp.int32)
    return (table, number)


def inverse_factor(noise, slot_scale):
    identity = jnp.eye(B, dtype=jnp.float32)
    return ((identity + noise * B ** (-0.5)) * slot_scale).astype(jnp.bfloat16)


def draw_inv_left(key, part):
    key = jax.random.fold_in(key, 3)
    shape = (N_DP, N_REPLICA, SLOTS, B, B)
    slot_scale = jnp.exp(jax.random.uniform(jax.random.fold_in(key, 21), (N_DP, N_REPLICA, SLOTS, 1, 1), jnp.float32, -0.7, 0.7))
    noise = 0.5 * jax.random.normal(key, shape, jnp.float32)
    return inverse_factor(noise, slot_scale)


def draw_inv_right(key, part):
    key = jax.random.fold_in(key, 5)
    shape = (N_DP, N_REPLICA, SLOTS, B, B)
    slot_scale = jnp.exp(jax.random.uniform(jax.random.fold_in(key, 23), (N_DP, N_REPLICA, SLOTS, 1, 1), jnp.float32, -0.7, 0.7))
    noise = 0.5 * jax.random.normal(key, shape, jnp.float32)
    return inverse_factor(noise, slot_scale)


def draw_gradients(key, part):
    key = jax.random.fold_in(key, 17)
    shape = (NBLK, B, B)
    block_scale = jnp.exp(jax.random.uniform(jax.random.fold_in(key, 31), (NBLK, 1, 1), jnp.float32, -1.2, 1.1))
    rising = jnp.exp(jnp.arange(B, dtype=jnp.float32) * (1.386 / (B - 1)))[None, :, None]
    noise = jnp.clip(0.25 * jax.random.normal(key, shape, jnp.float32), -1.5, 1.5)
    return (noise * block_scale * rising).astype(jnp.bfloat16)


def draw_owned_blocks(key, part):
    table, number = ownership(key)
    return table


def draw_owner_counts(key, part):
    table, number = ownership(key)
    return number


def touch_ends(values, stream_key, least, largest):
    dims = values.shape
    index_at = [jax.random.randint(jax.random.fold_in(stream_key, axis), (), 0, dims[axis]) for axis in range(len(dims))]
    values = values.at[tuple(index_at)].set(least)
    longest = dims.index(max(dims))
    index_at[longest] = (index_at[longest] + 1) % dims[longest]
    return values.at[tuple(index_at)].set(largest)


def shard_levels(stream_key, shape, pieces, low, largest):
    def one(dim, shards_of):
        steps = jax.random.uniform(jax.random.fold_in(jax.random.fold_in(stream_key, 6), dim), (shards_of,), jnp.float32, low / len(pieces), largest / len(pieces))
        return jnp.repeat(jnp.exp(steps), shape[dim] // shards_of).reshape((-1,) + (1,) * (len(shape) - dim - 1))

    factor_of = one(*pieces[0])
    for cut in pieces[1:]:
        factor_of = factor_of * one(*cut)
    return factor_of


def bell_draw(own_key, shape, scale, limit, split=(), kind=jnp.bfloat16):
    gain = shard_levels(own_key, shape, split, -0.22, 0.18) if split else 1.0
    values = jax.random.normal(own_key, shape, jnp.float32) * scale * gain
    return jnp.minimum(jnp.maximum(values, -limit), limit).astype(kind)


def setup_inputs(seed: int = 0) -> dict:
    streams_of = jax.random.split(jax.random.key(seed), 9)
    gradients = draw_gradients(jax.random.fold_in(streams_of[8], 71), 0)
    stat_left = bell_draw(streams_of[1], (NBLK, B, B), 1.0, 6.0, ((0, 32), (1, 4)), jnp.float32)
    stat_right = bell_draw(streams_of[2], (NBLK, B, B), 1.0, 6.0, ((0, 32), (1, 4)), jnp.float32)
    inv_left = draw_inv_left(jax.random.fold_in(streams_of[8], 71), 0)
    inv_right = draw_inv_right(jax.random.fold_in(streams_of[8], 71), 0)
    owned_blocks = draw_owned_blocks(jax.random.fold_in(streams_of[8], 71), 0)
    owner_counts = draw_owner_counts(jax.random.fold_in(streams_of[8], 71), 0)
    block_matrix = touch_ends(jax.random.randint(streams_of[7], (NBLK,), 0, NMAT), jax.random.fold_in(streams_of[7], 1), 0, NMAT - 1).astype(jnp.int32)
    return {"gradients": gradients, "stat_left": stat_left, "stat_right": stat_right, "inv_left": inv_left, "inv_right": inv_right, "owned_blocks": owned_blocks, "owner_counts": owner_counts, "block_matrix": block_matrix}


STAT_DECAY = 0.95
EPSILON = 1e-06

def slot_table(owned_blocks, owner_counts):
    slot_ids = jnp.arange(SLOTS, dtype=jnp.int32)
    live = slot_ids[None, None, :] < owner_counts[:, :, None]
    local_ids = jnp.arange(BLK_DP, dtype=jnp.int32)
    match = (owned_blocks[:, :, :, None] == local_ids[None, None, None, :]) & live[:, :, :, None]
    codes = (jnp.arange(N_REPLICA, dtype=jnp.int32)[:, None] * SLOTS + slot_ids[None, :]).astype(jnp.int32)
    within = lax.optimization_barrier(jnp.sum(jnp.where(match, codes[None, :, :, None], 0), axis=(1, 2))).astype(jnp.int32)
    offsets = (jnp.arange(N_DP, dtype=jnp.int32)[:, None] * (N_REPLICA * SLOTS)).astype(jnp.int32)
    return (within + offsets).reshape(NBLK).astype(jnp.int32)

def reference(gradients, stat_left, stat_right, inv_left, inv_right, owned_blocks, owner_counts, block_matrix):

    def statistics(items):
        block, left, right = items
        outer = jnp.dot(block, block.T, preferred_element_type=jnp.float32)
        inner = jnp.dot(block.T, block, preferred_element_type=jnp.float32)
        return (STAT_DECAY * left + (1.0 - STAT_DECAY) * outer, STAT_DECAY * right + (1.0 - STAT_DECAY) * inner)
    new_left, new_right = lax.map(statistics, (gradients, stat_left, stat_right))
    table = slot_table(owned_blocks, owner_counts)
    lefts = inv_left.reshape(N_DP * N_REPLICA * SLOTS, B, B)
    rights = inv_right.reshape(N_DP * N_REPLICA * SLOTS, B, B)

    def precondition(items):
        block, source = items
        left_factor = lax.dynamic_index_in_dim(lefts, source, 0, keepdims=False)
        right_factor = lax.dynamic_index_in_dim(rights, source, 0, keepdims=False)
        middle = jnp.dot(left_factor, block, preferred_element_type=jnp.float32).astype(jnp.bfloat16)
        return jnp.dot(middle, right_factor, preferred_element_type=jnp.float32).astype(jnp.bfloat16)
    precond = lax.map(precondition, (gradients, table))
    matrix_hot = (block_matrix[:, None] == jnp.arange(NMAT, dtype=jnp.int32)[None, :]).astype(jnp.float32)
    grad_sq = lax.optimization_barrier(jnp.sum(jnp.square(gradients.astype(jnp.float32)), axis=(1, 2)))
    pre_sq = lax.optimization_barrier(jnp.sum(jnp.square(precond.astype(jnp.float32)), axis=(1, 2)))
    grad_total = lax.optimization_barrier(jnp.sum(matrix_hot * grad_sq[:, None], axis=0))
    pre_total = lax.optimization_barrier(jnp.sum(matrix_hot * pre_sq[:, None], axis=0))
    graft = jnp.sqrt(grad_total) / jnp.sqrt(pre_total + EPSILON)
    block_scale = lax.optimization_barrier(jnp.sum(matrix_hot * graft[None, :], axis=1))
    update = (precond.astype(jnp.float32) * block_scale[:, None, None]).astype(jnp.bfloat16)
    return (update, new_left, new_right)
```

```python
import jax
import jax.numpy as jnp
from jax import lax
from jax.experimental import pallas as pl
from jax.experimental.pallas import tpu as pltpu
from jax.sharding import PartitionSpec as P

NMAT = 5
STAT_DECAY = 0.95
EPSILON = 1e-06
BF16 = jnp.bfloat16
F32 = jnp.float32
VMEM_LIMIT = 48 * 1024 * 1024
OFFSETS = (2, 1, 3, 0)


def shift(x, step):
    count = lax.axis_size("replica")
    return lax.ppermute(x, "replica", [(i, (i + step) % count) for i in range(count)])


def exchange(x, axis, bit):
    count = lax.axis_size(axis)
    return lax.ppermute(x, axis, [(i, i ^ bit) for i in range(count)])


def sum_everywhere(x):
    for axis in ("replica", "dp"):
        bit = 1
        while bit < lax.axis_size(axis):
            x = x + exchange(x, axis, bit)
            bit *= 2
    return x


def roots_kernel(info, left, block, right, *refs):
    outs, total, middle = refs[:7], refs[7], refs[8]
    step = pl.program_id(0)
    tiles = pl.num_programs(0) // 2
    rows = left.shape[1]
    owned = info[1] == 1

    @pl.when(step == 0)
    def _():
        total[...] = jnp.zeros_like(total)

    @pl.when(owned & (step < tiles))
    def _():
        product = jnp.dot(left[0], block[...], preferred_element_type=F32)
        middle[pl.ds(pl.multiple_of(step * rows, rows), rows), :] = product.astype(BF16)

    def quarter(place):
        half = middle.shape[0] // 2
        pieces = []
        for top in (0, half):
            product = jnp.dot(middle[top : top + half, :], right[0], preferred_element_type=F32)
            pieces.append(product.astype(BF16))
            wide = pieces[-1].astype(F32)
            squares = jnp.sum(jnp.square(wide).reshape(half // 8, 8, wide.shape[1]), axis=0)
            total[...] += squares[:, :128] + squares[:, 128:]
        if place < 3:
            outs[2 * place][...] = pieces[0]
            outs[2 * place + 1][...] = pieces[1]
        else:
            outs[6][:half, :] = pieces[0]
            outs[6][half:, :] = pieces[1]

    for place in range(4):
        pl.when(owned & (step == tiles + place))(lambda place=place: quarter(place))


def apply_roots(info, left, block, right):
    order = block.shape[0]
    tile = order // 4
    half = order // 2

    def left_map(step, info):
        return (info[0], jnp.where(info[1] == 1, jnp.minimum(step, 3), 0), 0)

    def right_map(step, info):
        place = jnp.maximum(step - 4, 0)
        offset = jnp.where(place == 0, 2, jnp.where(place == 1, 1, jnp.where(place == 2, 3, 0)))
        return (info[0], 0, jnp.where(info[1] == 1, lax.rem(info[2] + offset, 4), 0))

    whole = lambda step, info: (0, 0)
    piece = jax.ShapeDtypeStruct((half, tile), BF16)
    return pl.pallas_call(
        roots_kernel,
        out_shape=[piece] * 6
        + [jax.ShapeDtypeStruct((order, tile), BF16), jax.ShapeDtypeStruct((8, 128), F32)],
        grid_spec=pltpu.PrefetchScalarGridSpec(
            num_scalar_prefetch=1,
            grid=(8,),
            in_specs=[
                pl.BlockSpec((1, tile, order), left_map),
                pl.BlockSpec((order, order), whole),
                pl.BlockSpec((1, order, tile), right_map),
            ],
            out_specs=[pl.BlockSpec((half, tile), whole)] * 6
            + [pl.BlockSpec((order, tile), whole), pl.BlockSpec((8, 128), whole)],
            scratch_shapes=[pltpu.VMEM((order, order), BF16)],
        ),
        compiler_params=pltpu.CompilerParams(
            dimension_semantics=("arbitrary",), vmem_limit_bytes=VMEM_LIMIT
        ),
        cost_estimate=pl.CostEstimate(
            flops=4 * order**3, bytes_accessed=8 * order * order * 2, transcendentals=0
        ),
        name="roots",
    )(info, left, block, right)


def scale_kernel(which, slots, scales, place, *refs):
    ins, out = refs[:8], refs[-1]
    part, sub = pl.program_id(0), pl.program_id(1)
    count = out.shape[0]
    width = ins[0].shape[-1]
    base = (part * pl.num_programs(1) + sub) * count

    def write(sources):
        for i in range(count):
            factor = scales[(base + i) * slots + which]
            for source, offset in sources:
                column = pl.multiple_of(lax.rem(place[0] + offset, 4) * width, width)
                values = source[i].astype(F32) * factor
                out[i, 0, :, pl.ds(column, width)] = values.astype(BF16)

    @pl.when(part == 0)
    def _():
        write([(ins[0], 0), (ins[1], 3), (ins[2], 1), (ins[3], 2)])

    @pl.when(part == 1)
    def _():
        write([(ins[4], 0), (ins[5], 3), (ins[6], 1), (ins[7], 2)])


def scale_rows(which, slots, scales, place, low, high, earlier):
    half, rows, width = low[0].shape
    per_step = 8
    subs = half // per_step
    low_map = lambda part, sub: (jnp.where(part == 0, sub, subs - 1), 0, 0)
    high_map = lambda part, sub: (jnp.where(part == 1, sub, 0), 0, 0)
    smem = pl.BlockSpec(memory_space=pltpu.SMEM)
    block = (per_step, rows, width)
    operands = [scales, place, *low, *high]
    in_specs = (
        [smem, smem] + [pl.BlockSpec(block, low_map)] * 4 + [pl.BlockSpec(block, high_map)] * 4
    )
    aliases = {}
    if earlier is not None:
        aliases = {len(operands): 0}
        operands.append(earlier)
        in_specs.append(pl.BlockSpec(memory_space=pl.ANY))
    return pl.pallas_call(
        lambda *refs: scale_kernel(which, slots, *refs),
        out_shape=jax.ShapeDtypeStruct((2 * half, slots, rows, 4 * width), BF16),
        grid=(2, subs),
        in_specs=in_specs,
        out_specs=pl.BlockSpec(
            (per_step, 1, rows, 4 * width), lambda part, sub: (part * subs + sub, which, 0, 0)
        ),
        input_output_aliases=aliases,
        compiler_params=pltpu.CompilerParams(
            dimension_semantics=("arbitrary", "arbitrary"), vmem_limit_bytes=VMEM_LIMIT
        ),
        cost_estimate=pl.CostEstimate(
            flops=2 * half * rows * 4 * width,
            bytes_accessed=2 * 2 * half * rows * 4 * width * 2,
            transcendentals=0,
        ),
        name="scale",
    )(*operands)


def scatter_quarters(pieces, own, owner, me):
    far_low, far_high, right_low, right_high, left_low, left_high = pieces
    half = far_low.shape[0]
    mine = owner == me
    via_right = shift(far_low, 1)
    via_left = shift(far_high, -1)
    got_left_high = shift(right_high, 1)
    got_right_low = shift(left_low, -1)
    got_left_low = shift(jnp.where(mine, right_low, via_right), 1)
    got_right_high = shift(jnp.where(mine, left_high, via_left), -1)
    from_right = owner == lax.rem(me + 1, 4)
    from_left = owner == lax.rem(me + 3, 4)
    low = jnp.where(mine, own[:half], jnp.where(from_right, got_right_low, got_left_low))
    high = jnp.where(mine, own[half:], jnp.where(from_left, got_left_high, got_right_high))
    return jnp.concatenate([low, high], axis=0)


def gather_quarters(quarter):
    half = quarter.shape[0] // 2
    low, high = quarter[:half], quarter[half:]
    left_low = shift(low, 1)
    right_high = shift(high, -1)
    left_high = shift(high, 1)
    right_low = shift(low, -1)
    far_low = shift(left_low, 1)
    far_high = shift(right_high, -1)
    return (low, left_low, right_low, far_low), (high, left_high, right_high, far_high)


def per_device(
    gradients, stat_left, stat_right, inv_left, inv_right, owned_blocks, owner_counts, block_matrix
):
    dp_count = lax.axis_size("dp")
    owner_total = lax.axis_size("replica")
    dp_index = lax.axis_index("dp")
    me = lax.axis_index("replica")
    block_total, shard_rows, order = gradients.shape
    local_total = block_total // dp_count
    slot_total = inv_left.shape[2]
    width = order // owner_total
    matrix_ids = jnp.arange(NMAT, dtype=jnp.int32)
    matrix_hot = (block_matrix[:, None] == matrix_ids[None, :]).astype(F32)

    by_owner = gradients.reshape(dp_count, local_total, shard_rows, order)
    blocks = []
    for b in range(local_total):
        arrived = lax.all_to_all(by_owner[:, b], "dp", split_axis=0, concat_axis=0, tiled=True)
        blocks.append(arrived.reshape(order, order))

    grad_sq = jnp.sum(jnp.square(gradients.astype(F32)), axis=(1, 2))
    grad_part = jnp.sum(matrix_hot * grad_sq[:, None], axis=0)

    row_owned = lax.dynamic_index_in_dim(owned_blocks, dp_index, 0, keepdims=False)
    row_counts = lax.dynamic_index_in_dim(owner_counts, dp_index, 0, keepdims=False)
    slot_ids = jnp.arange(slot_total, dtype=jnp.int32)
    live = slot_ids[None, :] < row_counts[:, None]
    replica_ids = jnp.arange(owner_total, dtype=jnp.int32)

    quarters, pre_part = [], jnp.zeros((NMAT,), F32)
    for b in range(local_total):
        match = (row_owned == b) & live
        owner = jnp.sum(jnp.where(match, replica_ids[:, None], 0))
        slot = jnp.sum(jnp.where(match, slot_ids[None, :], 0))
        mine = owner == me
        info = jnp.stack([slot, mine.astype(jnp.int32), me]).astype(jnp.int32)
        *pieces, own, squares = apply_roots(info, inv_left[0, 0], blocks[b], inv_right[0, 0])
        number = lax.dynamic_index_in_dim(matrix_hot, dp_index * local_total + b, 0, keepdims=False)
        pre_part = pre_part + number * jnp.sum(squares)
        mixed = scatter_quarters(pieces, own, owner, me)
        quarters.append(
            lax.all_to_all(
                mixed.reshape(dp_count, shard_rows, width), "dp", split_axis=0, concat_axis=0, tiled=True
            )
        )

    parts = jnp.stack([pre_part, jnp.where(me == 0, grad_part, 0.0)])
    pre_total, grad_total = sum_everywhere(parts)
    graft = jnp.sqrt(grad_total) / jnp.sqrt(pre_total + EPSILON)
    scales = jnp.sum(matrix_hot * graft[None, :], axis=1)

    place = me.reshape(1).astype(jnp.int32)
    update = None
    for b in range(local_total):
        low, high = gather_quarters(quarters[b])
        update = scale_rows(b, local_total, scales, place, low, high, update)
    update = update.reshape(block_total, shard_rows, order)

    start = me * width
    left_parts, right_parts = [], []
    for b in range(local_total):
        rows = lax.dynamic_slice_in_dim(blocks[b], start, width, 0)
        columns = lax.dynamic_slice_in_dim(blocks[b], start, width, 1)
        left_parts.append(jnp.einsum("rk,ck->rc", rows, blocks[b], preferred_element_type=F32))
        right_parts.append(jnp.einsum("kr,kc->rc", columns, blocks[b], preferred_element_type=F32))
    new_left = STAT_DECAY * stat_left + (1.0 - STAT_DECAY) * jnp.stack(left_parts)
    new_right = STAT_DECAY * stat_right + (1.0 - STAT_DECAY) * jnp.stack(right_parts)
    return (update, new_left, new_right)


def solution(mesh):
    return jax.shard_map(
        per_device,
        mesh=mesh,
        in_specs=(
            P(None, "dp", None),
            P("dp", "replica", None),
            P("dp", "replica", None),
            P("dp", "replica", None, None, None),
            P("dp", "replica", None, None, None),
            P(),
            P(),
            P(),
        ),
        out_specs=(P(None, "dp", None), P("dp", "replica", None), P("dp", "replica", None)),
        check_vma=False,
    )
```

```python
import jax
import jax.numpy as jnp
from jax import lax
from jax.experimental import pallas as pl
from jax.experimental.pallas import tpu as pltpu
from jax.sharding import PartitionSpec as P

NMAT = 5
ORDER = ""
FRONT = "QD"
COSTS = (16, 24, 48, 8)
MERGED = False
STAT_DECAY = 0.95
EPSILON = 1e-06
BF16 = jnp.bfloat16
F32 = jnp.float32
VMEM_LIMIT = 60 * 1024 * 1024
EXTRA = 16
SUM_SCALE = 1.0 / 16.0


def params(steps=1):
    semantics = ("arbitrary",) * steps if steps else None
    return pltpu.CompilerParams(dimension_semantics=semantics, vmem_limit_bytes=VMEM_LIMIT)


def cost(flops, size):
    return pl.CostEstimate(flops=flops, bytes_accessed=size, transcendentals=0)


def shift(x, step):
    count = lax.axis_size("replica")
    return lax.ppermute(x, "replica", [(i, (i + step) % count) for i in range(count)])


def over_dp(x):
    return lax.all_to_all(x, "dp", split_axis=0, concat_axis=0, tiled=True)


def anywhere(count):
    return [pl.BlockSpec(memory_space=pl.ANY)] * count


SMEM = pl.BlockSpec(memory_space=pltpu.SMEM)


def pick_kernel(b, source, out, held, come, go):
    parts = come.shape[0]
    size = held.shape[0] // parts
    spans = [pl.ds(i * size, size) for i in range(parts)]
    reads = [
        pltpu.make_async_copy(source.at[span, b], held.at[span], come.at[i])
        for i, span in enumerate(spans)
    ]
    writes = [
        pltpu.make_async_copy(held.at[span], out.at[span], go.at[i]) for i, span in enumerate(spans)
    ]
    for read in reads:
        read.start()
    for read, write in zip(reads, writes):
        read.wait()
        write.start()
    for write in writes:
        write.wait()


def pick_block(by_owner, b, parts=8):
    count, _, rows, order = by_owner.shape
    return pl.pallas_call(
        lambda *refs: pick_kernel(b, *refs),
        out_shape=jax.ShapeDtypeStruct((count, rows, order), BF16),
        in_specs=anywhere(1),
        out_specs=anywhere(1)[0],
        scratch_shapes=[
            pltpu.VMEM((count, rows, order), BF16),
            pltpu.SemaphoreType.DMA((parts,)),
            pltpu.SemaphoreType.DMA((parts,)),
        ],
        compiler_params=params(0),
        cost_estimate=cost(0, COSTS[3] * count * rows * order),
        name="pick",
    )(by_owner)


def piece_places(me, pieces):
    count, _, width = pieces[0].shape
    for i, piece in enumerate(pieces):
        column = lax.rem(me + (0, 3, 1, 2, 2)[i], 4) * width
        first = count // 2 if i == 4 else 0
        yield piece, pl.ds(first, piece.shape[0]), pl.ds(pl.multiple_of(column, width), width)


def block_copies(me, which, pieces, block, sems):
    if len(pieces) == 1:
        source = pieces[0] if len(pieces[0].shape) == 3 else pieces[0].at[:, which]
        return [pltpu.make_async_copy(source, block, sems.at[0])]
    return [
        pltpu.make_async_copy(piece, block.at[chunks, :, columns], sems.at[i])
        for i, (piece, chunks, columns) in enumerate(piece_places(me, pieces))
    ]


def sum_squares(x):
    wide = x.astype(F32)
    return jnp.sum(jnp.square(wide).reshape(-1, 8, wide.shape[-1]), axis=0)


def split_sum(total, first, rows, shape):
    value = jnp.full(shape, jnp.sum(total) * SUM_SCALE, F32)
    out = jnp.zeros(shape, F32)
    for part in range(3):
        rounded = value.astype(BF16).astype(F32)
        out = jnp.where(rows == first + part, rounded, out)
        value = jnp.where(value == rounded, 0.0, value - rounded)
    return out


def roots_kernel(parts, last, info, left, right, *refs):
    pieces, refs = refs[:parts], refs[parts:]
    if last:
        before, refs = refs[0], refs[1:]
    outs, (block, left_held, right_held, middle, pre_sum, grad_sum, sems) = refs[:-7], refs[-7:]
    to_right, to_left, keep_right, keep_left, own = outs[:5]
    slot, owned, me = info[0], info[1] == 1, info[2]
    order = middle.shape[0]
    wide = order // 2
    width = order // 4
    pre_sum[...] = jnp.zeros_like(pre_sum)
    grad_sum[...] = jnp.zeros_like(grad_sum)

    @pl.when(owned)
    def _():
        first = block_copies(me, 1 if last else 0, pieces, block, sems)
        first.append(pltpu.make_async_copy(left.at[slot], left_held, sems.at[8]))
        second = []
        for place, offset in enumerate((2, 1, 3, 0)):
            column = pl.multiple_of(lax.rem(me + offset, 4) * width, width)
            source = right.at[slot, :, pl.ds(column, width)]
            target = right_held.at[:, pl.ds(place * width, width)]
            second.append(pltpu.make_async_copy(source, target, sems.at[9 + place]))
        for copy in first + second:
            copy.start()
        for copy in first:
            copy.wait()

        @pl.loop(0, 2)
        def _(i):
            columns = pl.ds(pl.multiple_of(i * wide, wide), wide)
            values = block[:, :, columns].reshape(order, wide)
            product = jnp.dot(left_held[...], values, preferred_element_type=F32)
            middle[:, columns] = product.astype(BF16)
            grad_sum[...] += sum_squares(values)

        for copy in second:
            copy.wait()
        for i in range(2):
            columns = slice(i * wide, (i + 1) * wide)
            product = jnp.dot(middle[...], right_held[:, columns], preferred_element_type=F32)
            product = product.astype(BF16)
            pre_sum[...] += sum_squares(product)
            chunks = product.reshape(block.shape[0], block.shape[1], wide)
            near, far = chunks[:, :, :width], chunks[:, :, width:]
            half = block.shape[0] // 2
            if i == 0:
                to_right[half : 2 * half] = near[:half]
                to_left[half : 2 * half] = near[half:]
                keep_right[:half] = far[:half]
                to_right[:half] = far[half:]
            else:
                to_left[:half] = near[:half]
                keep_left[:half] = near[half:]
                own[: 2 * half] = far

    shape = (block.shape[1], width)
    at = lax.broadcasted_iota(jnp.int32, shape, 0)
    extra = split_sum(pre_sum[...], 0, at, shape) + split_sum(grad_sum[...], 3, at, shape)
    if last:
        lane = lax.broadcasted_iota(jnp.int32, shape, 1)
        extra = jnp.where(lane < width // 2, before[...].astype(F32), extra).astype(BF16)
        for out in outs:
            out[out.shape[0] - 1] = extra
    else:
        outs[5][...] = extra.astype(BF16)


def apply_roots(info, left, pieces, right, before=None):
    order = left.shape[-1]
    width = order // 4
    rows = pieces[0].shape[-2]
    count = order // rows
    more = 0 if before is None else 1
    sizes = (count, count, count // 2, count // 2, count)
    shapes = [(size + more, rows, width) for size in sizes] + [(rows, width)] * (1 - more)
    operands = [info, left, right, *pieces]
    in_specs = [SMEM] + anywhere(len(operands) - 1)
    if before is not None:
        operands.append(before)
        in_specs.append(pl.BlockSpec(before.shape, lambda: (0, 0)))
    square = pltpu.VMEM((order, order), BF16)
    zeros = {2: lambda: (0, 0), 3: lambda: (0, 0, 0)}
    return pl.pallas_call(
        lambda *refs: roots_kernel(len(pieces), before is not None, *refs),
        out_shape=[jax.ShapeDtypeStruct(shape, BF16) for shape in shapes],
        in_specs=in_specs,
        out_specs=[pl.BlockSpec(shape, zeros[len(shape)]) for shape in shapes],
        scratch_shapes=[
            pltpu.VMEM((count, rows, order), BF16),
            square,
            square,
            square,
            pltpu.VMEM((8, order // 2), F32),
            pltpu.VMEM((8, order // 2), F32),
            pltpu.SemaphoreType.DMA((13,)),
        ],
        compiler_params=params(0),
        cost_estimate=cost(COSTS[0] * order**3, 10 * order * order),
        name="roots",
    )(*operands)


def stats_kernel(which, parts, info, *refs):
    pieces, (stat_left, stat_right), refs = refs[:parts], refs[parts : parts + 2], refs[parts + 2 :]
    new_left, new_right, block, turned, sems = refs[-5:]
    step = pl.program_id(0)
    width, order = turned.shape
    wide = new_left.shape[-1]
    rows = block.shape[1]
    start = pl.multiple_of(info[2] * width, width)
    span = width // rows

    @pl.when(step == 0)
    def _():
        copies = block_copies(info[2], which, pieces, block, sems)
        for copy in copies:
            copy.start()
        for copy in copies:
            copy.wait()
        turned[...] = block[:, :, pl.ds(start, width)].reshape(order, width).T

    mine = block[pl.ds(info[2] * span, span)].reshape(width, order)
    chunks = pl.ds(step * (wide // rows), wide // rows)
    others = block[chunks].reshape(wide, order)
    outer = lax.dot_general(mine, others, (((1,), (1,)), ((), ())), preferred_element_type=F32)
    new_left[0] = STAT_DECAY * stat_left[0] + (1.0 - STAT_DECAY) * outer
    columns = block[:, :, pl.ds(pl.multiple_of(step * wide, wide), wide)].reshape(order, wide)
    inner = jnp.dot(turned[...], columns, preferred_element_type=F32)
    new_right[0] = STAT_DECAY * stat_right[0] + (1.0 - STAT_DECAY) * inner


def update_stats(b, info, pieces, stat_left, stat_right, earlier, steps=2):
    _, rows, order = stat_left.shape
    spec = pl.BlockSpec((1, rows, order // steps), lambda step: (b, 0, step))
    operands = [info, *pieces, stat_left, stat_right]
    in_specs = [SMEM] + anywhere(len(pieces)) + [spec, spec]
    aliases = {}
    if earlier is not None:
        aliases = {len(operands): 0, len(operands) + 1: 1}
        operands += earlier
        in_specs += anywhere(2)
    chunk_rows = pieces[0].shape[-2]
    return pl.pallas_call(
        lambda *refs: stats_kernel(b, len(pieces), *refs),
        out_shape=[jax.ShapeDtypeStruct(stat_left.shape, F32)] * 2,
        grid=(steps,),
        in_specs=in_specs,
        out_specs=[spec, spec],
        scratch_shapes=[
            pltpu.VMEM((order // chunk_rows, chunk_rows, order), BF16),
            pltpu.VMEM((rows, order), BF16),
            pltpu.SemaphoreType.DMA((8,)),
        ],
        input_output_aliases=aliases,
        compiler_params=params(),
        cost_estimate=cost(COSTS[1] * rows * order**2, 2 * order * order + 16 * rows * order),
        name="stats",
    )(*operands)


def scale_kernel(which, slots, scales, place, *refs):
    pieces = refs[:5]
    out, held, ready, come, go = refs[-5:]
    half = pieces[4].shape[0]
    reads = []
    for part in range(2):
        for at in range(4):
            i = 4 * part + at
            source = pieces[3 + part] if at == 3 else pieces[at].at[pl.ds(part * half, half)]
            reads.append(pltpu.make_async_copy(source, held.at[i], come.at[i]))
    for read in reads:
        read.start()
    writes = []
    for part in range(2):
        for read in reads[4 * part : 4 * part + 4]:
            read.wait()
        for i in range(half):
            factor = scales[(part * half + i) * slots + which]
            for at, (_, _, columns) in enumerate(piece_places(place[0], pieces[:4])):
                values = held[4 * part + at, i].astype(F32) * factor
                ready[part * half + i, :, columns] = values.astype(BF16)
        span = pl.ds(part * half, half)
        writes.append(pltpu.make_async_copy(ready.at[span], out.at[span, which], go.at[part]))
        writes[-1].start()
    for write in writes:
        write.wait()


def scale_rows(which, slots, scales, place, pieces, earlier):
    count, rows, width = pieces[0].shape
    operands = [scales, place, *pieces] + ([] if earlier is None else [earlier])
    return pl.pallas_call(
        lambda *refs: scale_kernel(which, slots, *refs),
        out_shape=jax.ShapeDtypeStruct((count, slots, rows, 4 * width), BF16),
        in_specs=[SMEM, SMEM] + anywhere(len(operands) - 2),
        out_specs=anywhere(1)[0],
        scratch_shapes=[
            pltpu.VMEM((8, count // 2, rows, width), BF16),
            pltpu.VMEM((count, rows, 4 * width), BF16),
            pltpu.SemaphoreType.DMA((8,)),
            pltpu.SemaphoreType.DMA((2,)),
        ],
        input_output_aliases={} if earlier is None else {len(operands) - 1: 0},
        compiler_params=params(0),
        cost_estimate=cost(0, COSTS[2] * count * rows * width),
        name="scale",
    )(*operands)


def scale_both_kernel(scales, place, *refs):
    pieces = refs[:5]
    out, held, ready, come, go = refs[-5:]
    parts, _, size, _, width = held.shape
    slots = out.shape[1]
    rows = out.shape[2]
    reads = []
    for part in range(parts):
        for at in range(4):
            if at < 3:
                source = pieces[at].at[pl.ds(part * size, size)]
            else:
                source = pieces[3 + part // (parts // 2)].at[pl.ds(part % (parts // 2) * size, size)]
            reads.append(pltpu.make_async_copy(source, held.at[part, at], come.at[4 * part + at]))
    for read in reads:
        read.start()
    writes = []
    for part in range(parts):
        for read in reads[4 * part : 4 * part + 4]:
            read.wait()
        for i in range(size):
            for b in range(slots):
                factor = scales[(part * size + i) * slots + b]
                for at, (_, _, columns) in enumerate(piece_places(place[0], pieces[:4])):
                    values = held[part, at, i, b * rows : (b + 1) * rows].astype(F32) * factor
                    ready[part * size + i, b, :, columns] = values.astype(BF16)
        span = pl.ds(part * size, size)
        writes.append(pltpu.make_async_copy(ready.at[span], out.at[span], go.at[part]))
        writes[-1].start()
    for write in writes:
        write.wait()


def scale_both(scales, place, pieces, parts=4, slots=2):
    count, rows, width = pieces[0].shape
    shape = (count, slots, rows // slots, 4 * width)
    return pl.pallas_call(
        scale_both_kernel,
        out_shape=jax.ShapeDtypeStruct(shape, BF16),
        in_specs=[SMEM, SMEM] + anywhere(5),
        out_specs=anywhere(1)[0],
        scratch_shapes=[
            pltpu.VMEM((parts, 4, count // parts, rows, width), BF16),
            pltpu.VMEM(shape, BF16),
            pltpu.SemaphoreType.DMA((4 * parts,)),
            pltpu.SemaphoreType.DMA((parts,)),
        ],
        compiler_params=params(0),
        cost_estimate=cost(0, COSTS[2] * count * rows * width),
        name="scale",
    )(scales, place, *pieces)


def in_order(flag, first, *later):
    if flag not in ORDER:
        return (first, *later)
    return lax.optimization_barrier((first, *later))


def scatter_first(messages):
    return shift(messages[0], 1), shift(messages[1], -1)


def scatter_second(messages, first, mine):
    _, _, keep_right, keep_left, own = messages
    half = own.shape[0] // 2
    from_left, from_right = first
    return (
        shift(jnp.where(mine, keep_right, from_left[half:]), 1),
        shift(jnp.where(mine, keep_left, from_right[half:]), -1),
    )


def merge(messages, first, second, away):
    own, half = messages[4], messages[4].shape[0] // 2
    low = jnp.where(away == 1, first[1][:half], second[0][:half])
    low = jnp.where(away == 0, own[:half], low)
    high = jnp.where(away == 3, first[0][:half], second[1][:half])
    high = jnp.where(away == 0, own[half : 2 * half], high)
    return jnp.concatenate([low, high], axis=0)


def gather_first(quarter):
    return quarter, shift(quarter, 1), shift(quarter, -1)


def gather_second(pieces):
    _, left, right = pieces
    half = left.shape[0] // 2
    return [*pieces, shift(left[:half], 1), shift(right[half:], -1)]


def per_device(
    gradients, stat_left, stat_right, inv_left, inv_right, owned_blocks, owner_counts, block_matrix
):
    dp_count = lax.axis_size("dp")
    owner_total = lax.axis_size("replica")
    dp_index = lax.axis_index("dp")
    me = lax.axis_index("replica")
    block_total, shard_rows, order = gradients.shape
    local_total = block_total // dp_count
    slot_total = inv_left.shape[2]
    width = order // owner_total
    half = dp_count // 2

    by_owner = gradients.reshape(dp_count, local_total, shard_rows, order)
    if FRONT == "QD":
        my_columns = lax.dynamic_slice(
            by_owner, (0, 0, 0, me * width), (dp_count, 1, shard_rows, width)
        ).reshape(dp_count, shard_rows, width)
        arrived, late = in_order("p", over_dp(my_columns), by_owner)
        first_pieces = gather_first(arrived)
        second_block = over_dp(pick_block(late, 1))
        blocks = [gather_second(first_pieces), [second_block]]
    elif FRONT == "DD":
        picked = [pick_block(by_owner, b) for b in range(local_total)]
        arrived = over_dp(picked[0])
        arrived, picked[1] = in_order("p", arrived, picked[1])
        blocks = [[arrived], [over_dp(picked[1])]]
    else:
        arrived = over_dp(gradients).reshape(dp_count, local_total, shard_rows, order)
        blocks = [[arrived], [arrived]]

    slot_ids = jnp.arange(slot_total, dtype=jnp.int32)
    live = slot_ids[None, None, :] < owner_counts[:, :, None]
    replica_ids = jnp.arange(owner_total, dtype=jnp.int32)
    infos, owners = [], []
    for b in range(local_total):
        match = (owned_blocks == b) & live
        owners.append(jnp.sum(jnp.where(match, replica_ids[None, :, None], 0), axis=(1, 2)))
        slots = jnp.sum(jnp.where(match, slot_ids[None, None, :], 0), axis=(1, 2))
        owner = lax.dynamic_index_in_dim(owners[b], dp_index, 0, keepdims=False)
        slot = lax.dynamic_index_in_dim(slots, dp_index, 0, keepdims=False)
        away = lax.rem(owner - me + owner_total, owner_total)
        info = jnp.stack([slot, (away == 0).astype(jnp.int32), me, away])
        infos.append(info.astype(jnp.int32))

    away = [info[3] for info in infos]

    *sent, sums = apply_roots(infos[0], inv_left[0, 0], blocks[0], inv_right[0, 0])
    got = scatter_first(sent)
    sent_next = apply_roots(infos[1], inv_left[0, 0], blocks[1], inv_right[0, 0], sums)
    sent_next, got = in_order("r", sent_next, got)
    got_more = scatter_second(sent, got, away[0] == 0)
    got_more, sent_next = in_order("s", got_more, sent_next)
    got_next = scatter_first(sent_next)
    got_more, sent_next = in_order("m", got_more, sent_next)
    quarter = merge(sent, got, got_more, away[0])
    quarter, stat_left, stat_right = in_order("a", quarter, stat_left, stat_right)
    if not MERGED:
        first = over_dp(quarter)
        first, stat_left, stat_right = in_order("t", first, stat_left, stat_right)
        first, got_next = in_order("x", first, got_next)
    stats = update_stats(0, infos[0], blocks[0], stat_left, stat_right, None)
    stats, got_next = in_order("b", stats, got_next)

    chunk = lax.broadcasted_iota(jnp.int32, sent_next[2].shape, 0)
    lane = lax.broadcasted_iota(jnp.int32, sent_next[2].shape, 2)
    of_before = (chunk == half) & (lane < width // 2)
    got_next_more = scatter_second(sent_next, got_next, jnp.where(of_before, away[0], away[1]) == 0)
    far_off = jnp.where(of_before[half], away[0], away[1])
    sums = jnp.where(far_off == 1, got_next[1][2 * half], got_next_more[0][half])
    sums = jnp.where(far_off == 3, got_next[0][2 * half], sums)
    sums = jnp.where(far_off == 0, sent_next[4][2 * half], sums)
    sums = jnp.broadcast_to(sums[None, :EXTRA], (dp_count, EXTRA, width))
    stats, got_next_more = in_order("c", stats, got_next_more)
    stats = update_stats(1, infos[1], blocks[1], stat_left, stat_right, stats)
    quarter_next = merge(sent_next, got_next, got_next_more, away[1])
    stats, quarter_next = in_order("u", stats, quarter_next)
    if MERGED:
        second = over_dp(jnp.concatenate([quarter, quarter_next, sums], axis=1))
        stats, second = in_order("d", stats, second)
        both = gather_first(second[:, : 2 * shard_rows])
        far = gather_second(both)
        sums = second[:, 2 * shard_rows : 2 * shard_rows + 6, :].astype(F32)
    else:
        pieces = gather_first(first)
        pieces, quarter_next = in_order("y", pieces, quarter_next)
        second = over_dp(jnp.concatenate([quarter_next, sums], axis=1))
        pieces, second = in_order("v", pieces, second)
        gathered = gather_second(pieces)
        pieces_next = gather_first(second[:, :shard_rows])
        gathered, pieces_next = in_order("w", gathered, pieces_next)
        sums = second[:, shard_rows : shard_rows + 6, :].astype(F32)

    sums = sums.reshape(dp_count, 2, 3, local_total, width // local_total)[..., 0]
    sums = jnp.sum(sums, axis=2) / SUM_SCALE
    sums = jnp.swapaxes(sums, 1, 2).reshape(block_total, 2)

    matrix_ids = jnp.arange(NMAT, dtype=jnp.int32)
    matrix_hot = (block_matrix[:, None] == matrix_ids[None, :]).astype(F32)
    totals = jnp.sum(matrix_hot[:, :, None] * sums[:, None, :], axis=0)
    graft = jnp.sqrt(totals[:, 1]) / jnp.sqrt(totals[:, 0] + EPSILON)
    scales = jnp.sum(matrix_hot * graft[None, :], axis=1)

    place = me.reshape(1).astype(jnp.int32)
    if MERGED:
        update = scale_both(scales, place, far)
    else:
        update = scale_rows(0, local_total, scales, place, gathered, None)
        update, pieces_next = in_order("z", update, pieces_next)
        update = scale_rows(1, local_total, scales, place, gather_second(pieces_next), update)
    return (update.reshape(block_total, shard_rows, order), *stats)


def solution(mesh):
    return jax.shard_map(
        per_device,
        mesh=mesh,
        in_specs=(
            P(None, "dp", None),
            P("dp", "replica", None),
            P("dp", "replica", None),
            P("dp", "replica", None, None, None),
            P("dp", "replica", None, None, None),
            P(),
            P(),
            P(),
        ),
        out_specs=(P(None, "dp", None), P("dp", "replica", None), P("dp", "replica", None)),
        check_vma=False,
    )
```

```python
import jax
import jax.numpy as jnp
from jax import lax
from jax.experimental import pallas as pl
from jax.experimental.pallas import tpu as pltpu
from jax.sharding import PartitionSpec as P

NMAT = 5
STAT_DECAY = 0.95
EPSILON = 1e-06
BF16 = jnp.bfloat16
F32 = jnp.float32
EXTRA = 16
SUM_SCALE = 1.0 / 16.0


def params(steps=1, mib=60):
    semantics = ("arbitrary",) * steps if steps else None
    return pltpu.CompilerParams(dimension_semantics=semantics, vmem_limit_bytes=mib * 1024 * 1024)


def cost(flops, size):
    return pl.CostEstimate(flops=flops, bytes_accessed=size, transcendentals=0)


def shift(x, step):
    count = lax.axis_size("replica")
    return lax.ppermute(x, "replica", [(i, (i + step) % count) for i in range(count)])


def over_dp(x):
    return lax.all_to_all(x, "dp", split_axis=0, concat_axis=0, tiled=True)


def anywhere(count):
    return [pl.BlockSpec(memory_space=pl.ANY)] * count


SMEM = pl.BlockSpec(memory_space=pltpu.SMEM)


def pick_kernel(b, source, out, held, come, go):
    parts = come.shape[0]
    size = held.shape[0] // parts
    spans = [pl.ds(i * size, size) for i in range(parts)]
    reads = [
        pltpu.make_async_copy(source.at[span, b], held.at[span], come.at[i])
        for i, span in enumerate(spans)
    ]
    writes = [
        pltpu.make_async_copy(held.at[span], out.at[span], go.at[i]) for i, span in enumerate(spans)
    ]
    for read in reads:
        read.start()
    for read, write in zip(reads, writes):
        read.wait()
        write.start()
    for write in writes:
        write.wait()


def pick_block(by_owner, b, parts=8):
    count, _, rows, order = by_owner.shape
    return pl.pallas_call(
        lambda *refs: pick_kernel(b, *refs),
        out_shape=jax.ShapeDtypeStruct((count, rows, order), BF16),
        in_specs=anywhere(1),
        out_specs=anywhere(1)[0],
        scratch_shapes=[
            pltpu.VMEM((count, rows, order), BF16),
            pltpu.SemaphoreType.DMA((parts,)),
            pltpu.SemaphoreType.DMA((parts,)),
        ],
        compiler_params=params(0),
        cost_estimate=cost(0, 8 * count * rows * order),
        name="pick",
    )(by_owner)


def piece_places(me, pieces):
    count, _, width = pieces[0].shape
    for i, piece in enumerate(pieces):
        column = lax.rem(me + (0, 3, 1, 2, 2)[i], 4) * width
        first = count // 2 if i == 4 else 0
        yield piece, pl.ds(first, piece.shape[0]), pl.ds(pl.multiple_of(column, width), width)


def block_copies(me, pieces, block, sems):
    if len(pieces) == 1:
        return [pltpu.make_async_copy(pieces[0], block, sems.at[0])]
    return [
        pltpu.make_async_copy(piece, block.at[chunks, :, columns], sems.at[i])
        for i, (piece, chunks, columns) in enumerate(piece_places(me, pieces))
    ]


def sum_squares(x):
    wide = x.astype(F32)
    return jnp.sum(jnp.square(wide).reshape(-1, 8, wide.shape[-1]), axis=0)


def split_sum(total, first, rows, shape):
    value = jnp.full(shape, jnp.sum(total) * SUM_SCALE, F32)
    out = jnp.zeros(shape, F32)
    for part in range(3):
        rounded = value.astype(BF16).astype(F32)
        out = jnp.where(rows == first + part, rounded, out)
        value = jnp.where(value == rounded, 0.0, value - rounded)
    return out


def roots_kernel(parts, last, info, left, right, *refs):
    pieces, refs = refs[:parts], refs[parts:]
    if last:
        before, refs = refs[0], refs[1:]
    outs, (block, left_held, right_held, middle, pre_sum, grad_sum, sems) = refs[:-7], refs[-7:]
    to_right, to_left, keep_right, keep_left, own = outs[:5]
    slot, owned, me = info[0], info[1] == 1, info[2]
    order = middle.shape[0]
    wide = order // 2
    width = order // 4
    pre_sum[...] = jnp.zeros_like(pre_sum)
    grad_sum[...] = jnp.zeros_like(grad_sum)

    @pl.when(owned)
    def _():
        first = block_copies(me, pieces, block, sems)
        first.append(pltpu.make_async_copy(left.at[slot], left_held, sems.at[8]))
        second = []
        for place, offset in enumerate((2, 1, 3, 0)):
            column = pl.multiple_of(lax.rem(me + offset, 4) * width, width)
            source = right.at[slot, :, pl.ds(column, width)]
            target = right_held.at[:, pl.ds(place * width, width)]
            second.append(pltpu.make_async_copy(source, target, sems.at[9 + place]))
        for copy in first + second:
            copy.start()
        for copy in first:
            copy.wait()

        @pl.loop(0, 2)
        def _(i):
            columns = pl.ds(pl.multiple_of(i * wide, wide), wide)
            values = block[:, :, columns].reshape(order, wide)
            product = jnp.dot(left_held[...], values, preferred_element_type=F32)
            middle[:, columns] = product.astype(BF16)
            grad_sum[...] += sum_squares(values)

        for copy in second:
            copy.wait()
        for i in range(2):
            columns = slice(i * wide, (i + 1) * wide)
            product = jnp.dot(middle[...], right_held[:, columns], preferred_element_type=F32)
            product = product.astype(BF16)
            pre_sum[...] += sum_squares(product)
            chunks = product.reshape(block.shape[0], block.shape[1], wide)
            near, far = chunks[:, :, :width], chunks[:, :, width:]
            half = block.shape[0] // 2
            if i == 0:
                to_right[half : 2 * half] = near[:half]
                to_left[half : 2 * half] = near[half:]
                keep_right[:half] = far[:half]
                to_right[:half] = far[half:]
            else:
                to_left[:half] = near[:half]
                keep_left[:half] = near[half:]
                own[: 2 * half] = far

    shape = (block.shape[1], width)
    at = lax.broadcasted_iota(jnp.int32, shape, 0)
    extra = split_sum(pre_sum[...], 0, at, shape) + split_sum(grad_sum[...], 3, at, shape)
    if last:
        lane = lax.broadcasted_iota(jnp.int32, shape, 1)
        extra = jnp.where(lane < width // 2, before[...].astype(F32), extra).astype(BF16)
        for out in outs:
            out[out.shape[0] - 1] = extra
    else:
        outs[5][...] = extra.astype(BF16)


def apply_roots(info, left, pieces, right, before=None):
    order = left.shape[-1]
    width = order // 4
    rows = pieces[0].shape[-2]
    count = order // rows
    more = 0 if before is None else 1
    sizes = (count, count, count // 2, count // 2, count)
    shapes = [(size + more, rows, width) for size in sizes] + [(rows, width)] * (1 - more)
    operands = [info, left, right, *pieces]
    in_specs = [SMEM] + anywhere(len(operands) - 1)
    if before is not None:
        operands.append(before)
        in_specs.append(pl.BlockSpec(before.shape, lambda: (0, 0)))
    square = pltpu.VMEM((order, order), BF16)
    zeros = {2: lambda: (0, 0), 3: lambda: (0, 0, 0)}
    return pl.pallas_call(
        lambda *refs: roots_kernel(len(pieces), before is not None, *refs),
        out_shape=[jax.ShapeDtypeStruct(shape, BF16) for shape in shapes],
        in_specs=in_specs,
        out_specs=[pl.BlockSpec(shape, zeros[len(shape)]) for shape in shapes],
        scratch_shapes=[
            pltpu.VMEM((count, rows, order), BF16),
            square,
            square,
            square,
            pltpu.VMEM((8, order // 2), F32),
            pltpu.VMEM((8, order // 2), F32),
            pltpu.SemaphoreType.DMA((13,)),
        ],
        compiler_params=params(0, 50),
        cost_estimate=cost(16 * order**3, 10 * order * order),
        name="roots",
    )(*operands)


def stats_kernel(parts, info, *refs):
    pieces, (stat_left, stat_right), refs = refs[:parts], refs[parts : parts + 2], refs[parts + 2 :]
    new_left, new_right, block, turned, sems = refs[-5:]
    step = pl.program_id(0)
    width, order = turned.shape
    wide = new_left.shape[-1]
    rows = block.shape[1]
    start = pl.multiple_of(info[2] * width, width)
    span = width // rows

    @pl.when(step == 0)
    def _():
        copies = block_copies(info[2], pieces, block, sems)
        for copy in copies:
            copy.start()
        for copy in copies:
            copy.wait()
        turned[...] = block[:, :, pl.ds(start, width)].reshape(order, width).T

    mine = block[pl.ds(info[2] * span, span)].reshape(width, order)
    chunks = pl.ds(step * (wide // rows), wide // rows)
    others = block[chunks].reshape(wide, order)
    outer = lax.dot_general(mine, others, (((1,), (1,)), ((), ())), preferred_element_type=F32)
    new_left[0] = STAT_DECAY * stat_left[0] + (1.0 - STAT_DECAY) * outer
    columns = block[:, :, pl.ds(pl.multiple_of(step * wide, wide), wide)].reshape(order, wide)
    inner = jnp.dot(turned[...], columns, preferred_element_type=F32)
    new_right[0] = STAT_DECAY * stat_right[0] + (1.0 - STAT_DECAY) * inner


def update_stats(b, info, pieces, stat_left, stat_right, earlier, steps=2):
    _, rows, order = stat_left.shape
    spec = pl.BlockSpec((1, rows, order // steps), lambda step: (b, 0, step))
    operands = [info, *pieces, stat_left, stat_right]
    in_specs = [SMEM] + anywhere(len(pieces)) + [spec, spec]
    aliases = {}
    if earlier is not None:
        aliases = {len(operands): 0, len(operands) + 1: 1}
        operands += earlier
        in_specs += anywhere(2)
    chunk_rows = pieces[0].shape[-2]
    return pl.pallas_call(
        lambda *refs: stats_kernel(len(pieces), *refs),
        out_shape=[jax.ShapeDtypeStruct(stat_left.shape, F32)] * 2,
        grid=(steps,),
        in_specs=in_specs,
        out_specs=[spec, spec],
        scratch_shapes=[
            pltpu.VMEM((order // chunk_rows, chunk_rows, order), BF16),
            pltpu.VMEM((rows, order), BF16),
            pltpu.SemaphoreType.DMA((8,)),
        ],
        input_output_aliases=aliases,
        compiler_params=params(),
        cost_estimate=cost(24 * rows * order**2, 2 * order * order + 16 * rows * order),
        name="stats",
    )(*operands)


def scale_kernel(which, slots, scales, place, *refs):
    pieces = refs[:5]
    out, held, ready, come, go = refs[-5:]
    half = pieces[4].shape[0]
    reads = []
    for part in range(2):
        for at in range(4):
            i = 4 * part + at
            source = pieces[3 + part] if at == 3 else pieces[at].at[pl.ds(part * half, half)]
            reads.append(pltpu.make_async_copy(source, held.at[i], come.at[i]))
    for read in reads:
        read.start()
    writes = []
    for part in range(2):
        for read in reads[4 * part : 4 * part + 4]:
            read.wait()
        for i in range(half):
            factor = scales[(part * half + i) * slots + which]
            for at, (_, _, columns) in enumerate(piece_places(place[0], pieces[:4])):
                values = held[4 * part + at, i].astype(F32) * factor
                ready[part * half + i, :, columns] = values.astype(BF16)
        span = pl.ds(part * half, half)
        writes.append(pltpu.make_async_copy(ready.at[span], out.at[span, which], go.at[part]))
        writes[-1].start()
    for write in writes:
        write.wait()


def scale_rows(which, slots, scales, place, pieces, earlier):
    count, rows, width = pieces[0].shape
    operands = [scales, place, *pieces] + ([] if earlier is None else [earlier])
    return pl.pallas_call(
        lambda *refs: scale_kernel(which, slots, *refs),
        out_shape=jax.ShapeDtypeStruct((count, slots, rows, 4 * width), BF16),
        in_specs=[SMEM, SMEM] + anywhere(len(operands) - 2),
        out_specs=anywhere(1)[0],
        scratch_shapes=[
            pltpu.VMEM((8, count // 2, rows, width), BF16),
            pltpu.VMEM((count, rows, 4 * width), BF16),
            pltpu.SemaphoreType.DMA((8,)),
            pltpu.SemaphoreType.DMA((2,)),
        ],
        input_output_aliases={} if earlier is None else {len(operands) - 1: 0},
        compiler_params=params(0, 50),
        cost_estimate=cost(0, 48 * count * rows * width),
        name="scale",
    )(*operands)


def scatter_first(messages):
    return shift(messages[0], 1), shift(messages[1], -1)


def choose_second(messages, first, mine):
    _, _, keep_right, keep_left, own = messages
    half = own.shape[0] // 2
    from_left, from_right = first
    return jnp.where(mine, keep_right, from_left[half:]), jnp.where(mine, keep_left, from_right[half:])


def scatter_second(chosen):
    return shift(chosen[0], 1), shift(chosen[1], -1)


def merge(messages, first, second, away):
    own, half = messages[4], messages[4].shape[0] // 2
    low = jnp.where(away == 1, first[1][:half], second[0][:half])
    low = jnp.where(away == 0, own[:half], low)
    high = jnp.where(away == 3, first[0][:half], second[1][:half])
    high = jnp.where(away == 0, own[half : 2 * half], high)
    return jnp.concatenate([low, high], axis=0)


def gather_first(quarter):
    return quarter, shift(quarter, 1), shift(quarter, -1)


def gather_second(pieces):
    _, left, right = pieces
    half = left.shape[0] // 2
    return [*pieces, shift(left[:half], 1), shift(right[half:], -1)]


def per_device(
    gradients, stat_left, stat_right, inv_left, inv_right, owned_blocks, owner_counts, block_matrix
):
    dp_count = lax.axis_size("dp")
    owner_total = lax.axis_size("replica")
    dp_index = lax.axis_index("dp")
    me = lax.axis_index("replica")
    block_total, shard_rows, order = gradients.shape
    local_total = block_total // dp_count
    slot_total = inv_left.shape[2]
    width = order // owner_total
    half = dp_count // 2

    by_owner = gradients.reshape(dp_count, local_total, shard_rows, order)
    my_columns = lax.dynamic_slice(
        by_owner, (0, 0, 0, me * width), (dp_count, 1, shard_rows, width)
    ).reshape(dp_count, shard_rows, width)
    first_pieces = gather_first(over_dp(my_columns))
    second_block = over_dp(pick_block(by_owner, 1))
    blocks = [gather_second(first_pieces), [second_block]]

    slot_ids = jnp.arange(slot_total, dtype=jnp.int32)
    live = slot_ids[None, None, :] < owner_counts[:, :, None]
    replica_ids = jnp.arange(owner_total, dtype=jnp.int32)
    infos, owners = [], []
    for b in range(local_total):
        match = (owned_blocks == b) & live
        owners.append(jnp.sum(jnp.where(match, replica_ids[None, :, None], 0), axis=(1, 2)))
        slots = jnp.sum(jnp.where(match, slot_ids[None, None, :], 0), axis=(1, 2))
        owner = lax.dynamic_index_in_dim(owners[b], dp_index, 0, keepdims=False)
        slot = lax.dynamic_index_in_dim(slots, dp_index, 0, keepdims=False)
        away = lax.rem(owner - me + owner_total, owner_total)
        info = jnp.stack([slot, (away == 0).astype(jnp.int32), me, away])
        infos.append(info.astype(jnp.int32))

    away = [info[3] for info in infos]

    *sent, sums = apply_roots(infos[0], inv_left[0, 0], blocks[0], inv_right[0, 0])
    got = scatter_first(sent)
    sent_next = apply_roots(infos[1], inv_left[0, 0], blocks[1], inv_right[0, 0], sums)
    got_more = scatter_second(choose_second(sent, got, away[0] == 0))
    got_next = scatter_first(sent_next)
    first = over_dp(merge(sent, got, got_more, away[0]))
    stats = update_stats(0, infos[0], blocks[0], stat_left, stat_right, None)

    chunk = lax.broadcasted_iota(jnp.int32, sent_next[2].shape, 0)
    lane = lax.broadcasted_iota(jnp.int32, sent_next[2].shape, 2)
    of_before = (chunk == half) & (lane < width // 2)
    mine = jnp.where(of_before, away[0], away[1]) == 0
    got_next_more = scatter_second(choose_second(sent_next, got_next, mine))
    far_off = jnp.where(of_before[half], away[0], away[1])
    sums = jnp.where(far_off == 1, got_next[1][2 * half], got_next_more[0][half])
    sums = jnp.where(far_off == 3, got_next[0][2 * half], sums)
    sums = jnp.where(far_off == 0, sent_next[4][2 * half], sums)
    sums = jnp.broadcast_to(sums[None, :EXTRA], (dp_count, EXTRA, width))
    stats = update_stats(1, infos[1], blocks[1], stat_left, stat_right, stats)
    quarter = merge(sent_next, got_next, got_next_more, away[1])
    second = over_dp(jnp.concatenate([quarter, sums], axis=1))

    gathered = gather_second(gather_first(first))
    pieces_next = gather_first(second[:, :shard_rows])
    sums = second[:, shard_rows : shard_rows + 6, :].astype(F32)
    sums = sums.reshape(dp_count, 2, 3, local_total, width // local_total)[..., 0]
    sums = jnp.sum(sums, axis=2) / SUM_SCALE
    sums = jnp.swapaxes(sums, 1, 2).reshape(block_total, 2)

    matrix_ids = jnp.arange(NMAT, dtype=jnp.int32)
    matrix_hot = (block_matrix[:, None] == matrix_ids[None, :]).astype(F32)
    totals = jnp.sum(matrix_hot[:, :, None] * sums[:, None, :], axis=0)
    graft = jnp.sqrt(totals[:, 1]) / jnp.sqrt(totals[:, 0] + EPSILON)
    scales = jnp.sum(matrix_hot * graft[None, :], axis=1)

    place = me.reshape(1).astype(jnp.int32)
    update = scale_rows(0, local_total, scales, place, gathered, None)
    update = scale_rows(1, local_total, scales, place, gather_second(pieces_next), update)
    return (update.reshape(block_total, shard_rows, order), *stats)


def solution(mesh):
    return jax.shard_map(
        per_device,
        mesh=mesh,
        in_specs=(
            P(None, "dp", None),
            P("dp", "replica", None),
            P("dp", "replica", None),
            P("dp", "replica", None, None, None),
            P("dp", "replica", None, None, None),
            P(),
            P(),
            P(),
        ),
        out_specs=(P(None, "dp", None), P("dp", "replica", None), P("dp", "replica", None)),
        check_vma=False,
    )
```

```python
import jax
import jax.numpy as jnp
from jax import lax
from jax.experimental import pallas as pl
from jax.experimental.pallas import tpu as pltpu
from jax.sharding import PartitionSpec as P

NMAT = 5
STAT_DECAY = 0.95
EPSILON = 1e-06
BF16 = jnp.bfloat16
F32 = jnp.float32
EXTRA = 16
SUM_SCALE = 1.0 / 16.0


def params(steps=1, mib=60):
    semantics = ("arbitrary",) * steps if steps else None
    return pltpu.CompilerParams(dimension_semantics=semantics, vmem_limit_bytes=mib * 1024 * 1024)


def cost(flops, size):
    return pl.CostEstimate(flops=flops, bytes_accessed=size, transcendentals=0)


def shift(x, step):
    count = lax.axis_size("replica")
    return lax.ppermute(x, "replica", [(i, (i + step) % count) for i in range(count)])


def over_dp(x):
    return lax.all_to_all(x, "dp", split_axis=0, concat_axis=0, tiled=True)


def anywhere(count):
    return [pl.BlockSpec(memory_space=pl.ANY)] * count


SMEM = pl.BlockSpec(memory_space=pltpu.SMEM)


def pick_kernel(b, source, out, held, come, go):
    parts = come.shape[0]
    size = held.shape[0] // parts
    spans = [pl.ds(i * size, size) for i in range(parts)]
    reads = [
        pltpu.make_async_copy(source.at[span, b], held.at[span], come.at[i])
        for i, span in enumerate(spans)
    ]
    writes = [
        pltpu.make_async_copy(held.at[span], out.at[span], go.at[i]) for i, span in enumerate(spans)
    ]
    for read in reads:
        read.start()
    for read, write in zip(reads, writes):
        read.wait()
        write.start()
    for write in writes:
        write.wait()


def pick_block(by_owner, b, parts=8):
    count, _, rows, order = by_owner.shape
    return pl.pallas_call(
        lambda *refs: pick_kernel(b, *refs),
        out_shape=jax.ShapeDtypeStruct((count, rows, order), BF16),
        in_specs=anywhere(1),
        out_specs=anywhere(1)[0],
        scratch_shapes=[
            pltpu.VMEM((count, rows, order), BF16),
            pltpu.SemaphoreType.DMA((parts,)),
            pltpu.SemaphoreType.DMA((parts,)),
        ],
        compiler_params=params(0),
        cost_estimate=cost(0, 8 * count * rows * order),
        name="pick",
    )(by_owner)


def piece_places(me, pieces):
    count, _, width = pieces[0].shape
    for i, piece in enumerate(pieces):
        column = lax.rem(me + (0, 3, 1, 2, 2)[i], 4) * width
        first = count // 2 if i == 4 else 0
        yield piece, pl.ds(first, piece.shape[0]), pl.ds(pl.multiple_of(column, width), width)


def block_copies(me, pieces, block, sems):
    if len(pieces) == 1:
        return [pltpu.make_async_copy(pieces[0], block, sems.at[0])]
    return [
        pltpu.make_async_copy(piece, block.at[chunks, :, columns], sems.at[i])
        for i, (piece, chunks, columns) in enumerate(piece_places(me, pieces))
    ]


def sum_squares(x):
    wide = x.astype(F32)
    return jnp.sum(jnp.square(wide).reshape(-1, 8, wide.shape[-1]), axis=0)


def split_sum(total, first, rows, shape):
    value = jnp.full(shape, jnp.sum(total) * SUM_SCALE, F32)
    out = jnp.zeros(shape, F32)
    for part in range(3):
        rounded = value.astype(BF16).astype(F32)
        out = jnp.where(rows == first + part, rounded, out)
        value = jnp.where(value == rounded, 0.0, value - rounded)
    return out


def roots_kernel(parts, last, info, left, right, *refs):
    pieces, refs = refs[:parts], refs[parts:]
    if last:
        before, refs = refs[0], refs[1:]
    outs, (block, left_held, right_held, middle, pre_sum, grad_sum, sems) = refs[:-7], refs[-7:]
    to_right, to_left, keep_right, keep_left, own = outs[:5]
    slot, owned, me = info[0], info[1] == 1, info[2]
    order = middle.shape[0]
    wide = order // 2
    width = order // 4
    pre_sum[...] = jnp.zeros_like(pre_sum)
    grad_sum[...] = jnp.zeros_like(grad_sum)

    @pl.when(owned)
    def _():
        first = block_copies(me, pieces, block, sems)
        first.append(pltpu.make_async_copy(left.at[slot], left_held, sems.at[8]))
        second = []
        for place, offset in enumerate((2, 1, 3, 0)):
            column = pl.multiple_of(lax.rem(me + offset, 4) * width, width)
            source = right.at[slot, :, pl.ds(column, width)]
            target = right_held.at[:, pl.ds(place * width, width)]
            second.append(pltpu.make_async_copy(source, target, sems.at[9 + place]))
        for copy in first + second:
            copy.start()
        for copy in first:
            copy.wait()

        @pl.loop(0, 2)
        def _(i):
            columns = pl.ds(pl.multiple_of(i * wide, wide), wide)
            values = block[:, :, columns].reshape(order, wide)
            product = jnp.dot(left_held[...], values, preferred_element_type=F32)
            middle[:, columns] = product.astype(BF16)
            grad_sum[...] += sum_squares(values)

        for copy in second:
            copy.wait()
        for i in range(2):
            columns = slice(i * wide, (i + 1) * wide)
            product = jnp.dot(middle[...], right_held[:, columns], preferred_element_type=F32)
            product = product.astype(BF16)
            pre_sum[...] += sum_squares(product)
            chunks = product.reshape(block.shape[0], block.shape[1], wide)
            near, far = chunks[:, :, :width], chunks[:, :, width:]
            half = block.shape[0] // 2
            if i == 0:
                to_right[half : 2 * half] = near[:half]
                to_left[half : 2 * half] = near[half:]
                keep_right[:half] = far[:half]
                to_right[:half] = far[half:]
            else:
                to_left[:half] = near[:half]
                keep_left[:half] = near[half:]
                own[: 2 * half] = far

    shape = (block.shape[1], width)
    at = lax.broadcasted_iota(jnp.int32, shape, 0)
    extra = split_sum(pre_sum[...], 0, at, shape) + split_sum(grad_sum[...], 3, at, shape)
    if last:
        lane = lax.broadcasted_iota(jnp.int32, shape, 1)
        extra = jnp.where(lane < width // 2, before[...].astype(F32), extra).astype(BF16)
        for out in outs:
            out[out.shape[0] - 1] = extra
    else:
        outs[5][...] = extra.astype(BF16)


def apply_roots(info, left, pieces, right, before=None):
    order = left.shape[-1]
    width = order // 4
    rows = pieces[0].shape[-2]
    count = order // rows
    more = 0 if before is None else 1
    sizes = (count, count, count // 2, count // 2, count)
    shapes = [(size + more, rows, width) for size in sizes] + [(rows, width)] * (1 - more)
    operands = [info, left, right, *pieces]
    in_specs = [SMEM] + anywhere(len(operands) - 1)
    if before is not None:
        operands.append(before)
        in_specs.append(pl.BlockSpec(before.shape, lambda: (0, 0)))
    square = pltpu.VMEM((order, order), BF16)
    zeros = {2: lambda: (0, 0), 3: lambda: (0, 0, 0)}
    return pl.pallas_call(
        lambda *refs: roots_kernel(len(pieces), before is not None, *refs),
        out_shape=[jax.ShapeDtypeStruct(shape, BF16) for shape in shapes],
        in_specs=in_specs,
        out_specs=[pl.BlockSpec(shape, zeros[len(shape)]) for shape in shapes],
        scratch_shapes=[
            pltpu.VMEM((count, rows, order), BF16),
            square,
            square,
            square,
            pltpu.VMEM((8, order // 2), F32),
            pltpu.VMEM((8, order // 2), F32),
            pltpu.SemaphoreType.DMA((13,)),
        ],
        compiler_params=params(0, 50),
        cost_estimate=cost(16 * order**3, 10 * order * order),
        name="roots",
    )(*operands)


def stats_kernel(parts, info, *refs):
    pieces, (stat_left, stat_right), refs = refs[:parts], refs[parts : parts + 2], refs[parts + 2 :]
    new_left, new_right, block, turned, sems = refs[-5:]
    step = pl.program_id(0)
    width, order = turned.shape
    wide = new_left.shape[-1]
    rows = block.shape[1]
    start = pl.multiple_of(info[2] * width, width)
    span = width // rows

    @pl.when(step == 0)
    def _():
        copies = block_copies(info[2], pieces, block, sems)
        for copy in copies:
            copy.start()
        for copy in copies:
            copy.wait()
        turned[...] = block[:, :, pl.ds(start, width)].reshape(order, width).T

    mine = block[pl.ds(info[2] * span, span)].reshape(width, order)
    chunks = pl.ds(step * (wide // rows), wide // rows)
    others = block[chunks].reshape(wide, order)
    outer = lax.dot_general(mine, others, (((1,), (1,)), ((), ())), preferred_element_type=F32)
    new_left[0] = STAT_DECAY * stat_left[0] + (1.0 - STAT_DECAY) * outer
    columns = block[:, :, pl.ds(pl.multiple_of(step * wide, wide), wide)].reshape(order, wide)
    inner = jnp.dot(turned[...], columns, preferred_element_type=F32)
    new_right[0] = STAT_DECAY * stat_right[0] + (1.0 - STAT_DECAY) * inner


def update_stats(b, info, pieces, stat_left, stat_right, earlier, steps=2):
    _, rows, order = stat_left.shape
    spec = pl.BlockSpec((1, rows, order // steps), lambda step: (b, 0, step))
    operands = [info, *pieces, stat_left, stat_right]
    in_specs = [SMEM] + anywhere(len(pieces)) + [spec, spec]
    aliases = {}
    if earlier is not None:
        aliases = {len(operands): 0, len(operands) + 1: 1}
        operands += earlier
        in_specs += anywhere(2)
    chunk_rows = pieces[0].shape[-2]
    return pl.pallas_call(
        lambda *refs: stats_kernel(len(pieces), *refs),
        out_shape=[jax.ShapeDtypeStruct(stat_left.shape, F32)] * 2,
        grid=(steps,),
        in_specs=in_specs,
        out_specs=[spec, spec],
        scratch_shapes=[
            pltpu.VMEM((order // chunk_rows, chunk_rows, order), BF16),
            pltpu.VMEM((rows, order), BF16),
            pltpu.SemaphoreType.DMA((8,)),
        ],
        input_output_aliases=aliases,
        compiler_params=params(),
        cost_estimate=cost(24 * rows * order**2, 2 * order * order + 16 * rows * order),
        name="stats",
    )(*operands)


def scale_kernel(which, slots, scales, place, *refs):
    pieces = refs[:5]
    out, held, ready, come, go = refs[-5:]
    half = pieces[4].shape[0]
    reads = []
    for part in range(2):
        for at in range(4):
            i = 4 * part + at
            source = pieces[3 + part] if at == 3 else pieces[at].at[pl.ds(part * half, half)]
            reads.append(pltpu.make_async_copy(source, held.at[i], come.at[i]))
    for read in reads:
        read.start()
    writes = []
    for part in range(2):
        for read in reads[4 * part : 4 * part + 4]:
            read.wait()
        for i in range(half):
            factor = scales[(part * half + i) * slots + which]
            for at, (_, _, columns) in enumerate(piece_places(place[0], pieces[:4])):
                values = held[4 * part + at, i].astype(F32) * factor
                ready[part * half + i, :, columns] = values.astype(BF16)
        span = pl.ds(part * half, half)
        writes.append(pltpu.make_async_copy(ready.at[span], out.at[span, which], go.at[part]))
        writes[-1].start()
    for write in writes:
        write.wait()


def scale_rows(which, slots, scales, place, pieces, earlier):
    count, rows, width = pieces[0].shape
    operands = [scales, place, *pieces] + ([] if earlier is None else [earlier])
    return pl.pallas_call(
        lambda *refs: scale_kernel(which, slots, *refs),
        out_shape=jax.ShapeDtypeStruct((count, slots, rows, 4 * width), BF16),
        in_specs=[SMEM, SMEM] + anywhere(len(operands) - 2),
        out_specs=anywhere(1)[0],
        scratch_shapes=[
            pltpu.VMEM((8, count // 2, rows, width), BF16),
            pltpu.VMEM((count, rows, 4 * width), BF16),
            pltpu.SemaphoreType.DMA((8,)),
            pltpu.SemaphoreType.DMA((2,)),
        ],
        input_output_aliases={} if earlier is None else {len(operands) - 1: 0},
        compiler_params=params(0, 50),
        cost_estimate=cost(0, 48 * count * rows * width),
        name="scale",
    )(*operands)


def in_order(first, *later):
    return lax.optimization_barrier((first, *later))


def scatter_first(messages):
    return shift(messages[0], 1), shift(messages[1], -1)


def choose_second(messages, first, mine):
    _, _, keep_right, keep_left, own = messages
    half = own.shape[0] // 2
    from_left, from_right = first
    return jnp.where(mine, keep_right, from_left[half:]), jnp.where(mine, keep_left, from_right[half:])


def scatter_second(chosen):
    return shift(chosen[0], 1), shift(chosen[1], -1)


def merge(messages, first, second, away):
    own, half = messages[4], messages[4].shape[0] // 2
    low = jnp.where(away == 1, first[1][:half], second[0][:half])
    low = jnp.where(away == 0, own[:half], low)
    high = jnp.where(away == 3, first[0][:half], second[1][:half])
    high = jnp.where(away == 0, own[half : 2 * half], high)
    return jnp.concatenate([low, high], axis=0)


def gather_first(quarter):
    return quarter, shift(quarter, 1), shift(quarter, -1)


def gather_second(pieces):
    _, left, right = pieces
    half = left.shape[0] // 2
    return [*pieces, shift(left[:half], 1), shift(right[half:], -1)]


def per_device(
    gradients, stat_left, stat_right, inv_left, inv_right, owned_blocks, owner_counts, block_matrix
):
    dp_count = lax.axis_size("dp")
    owner_total = lax.axis_size("replica")
    dp_index = lax.axis_index("dp")
    me = lax.axis_index("replica")
    block_total, shard_rows, order = gradients.shape
    local_total = block_total // dp_count
    slot_total = inv_left.shape[2]
    width = order // owner_total
    half = dp_count // 2

    by_owner = gradients.reshape(dp_count, local_total, shard_rows, order)
    my_columns = lax.dynamic_slice(
        by_owner, (0, 0, 0, me * width), (dp_count, 1, shard_rows, width)
    ).reshape(dp_count, shard_rows, width)
    first_pieces = gather_first(over_dp(my_columns))
    second_block = over_dp(pick_block(by_owner, 1))
    blocks = [gather_second(first_pieces), [second_block]]

    slot_ids = jnp.arange(slot_total, dtype=jnp.int32)
    live = slot_ids[None, None, :] < owner_counts[:, :, None]
    replica_ids = jnp.arange(owner_total, dtype=jnp.int32)
    infos, owners = [], []
    for b in range(local_total):
        match = (owned_blocks == b) & live
        owners.append(jnp.sum(jnp.where(match, replica_ids[None, :, None], 0), axis=(1, 2)))
        slots = jnp.sum(jnp.where(match, slot_ids[None, None, :], 0), axis=(1, 2))
        owner = lax.dynamic_index_in_dim(owners[b], dp_index, 0, keepdims=False)
        slot = lax.dynamic_index_in_dim(slots, dp_index, 0, keepdims=False)
        away = lax.rem(owner - me + owner_total, owner_total)
        info = jnp.stack([slot, (away == 0).astype(jnp.int32), me, away])
        infos.append(info.astype(jnp.int32))

    away = [info[3] for info in infos]

    *sent, sums = apply_roots(infos[0], inv_left[0, 0], blocks[0], inv_right[0, 0])
    got = scatter_first(sent)
    sent_next = apply_roots(infos[1], inv_left[0, 0], blocks[1], inv_right[0, 0], sums)
    sent_next, got = in_order(sent_next, got)
    got_more = scatter_second(choose_second(sent, got, away[0] == 0))
    got_next = scatter_first(sent_next)
    first = over_dp(merge(sent, got, got_more, away[0]))

    chunk = lax.broadcasted_iota(jnp.int32, sent_next[2].shape, 0)
    lane = lax.broadcasted_iota(jnp.int32, sent_next[2].shape, 2)
    of_before = (chunk == half) & (lane < width // 2)
    mine = jnp.where(of_before, away[0], away[1]) == 0
    got_next_more = scatter_second(choose_second(sent_next, got_next, mine))
    far_off = jnp.where(of_before[half], away[0], away[1])
    sums = jnp.where(far_off == 1, got_next[1][2 * half], got_next_more[0][half])
    sums = jnp.where(far_off == 3, got_next[0][2 * half], sums)
    sums = jnp.where(far_off == 0, sent_next[4][2 * half], sums)
    sums = jnp.broadcast_to(sums[None, :EXTRA], (dp_count, EXTRA, width))
    quarter = merge(sent_next, got_next, got_next_more, away[1])
    second = over_dp(jnp.concatenate([quarter, sums], axis=1))

    pieces = gather_first(first)
    pieces, stat_left, stat_right = in_order(pieces, stat_left, stat_right)
    stats = update_stats(0, infos[0], blocks[0], stat_left, stat_right, None)
    stats = update_stats(1, infos[1], blocks[1], stat_left, stat_right, stats)
    gathered = gather_second(pieces)
    pieces_next = gather_first(second[:, :shard_rows])
    sums = second[:, shard_rows : shard_rows + 6, :].astype(F32)
    sums = sums.reshape(dp_count, 2, 3, local_total, width // local_total)[..., 0]
    sums = jnp.sum(sums, axis=2) / SUM_SCALE
    sums = jnp.swapaxes(sums, 1, 2).reshape(block_total, 2)

    matrix_ids = jnp.arange(NMAT, dtype=jnp.int32)
    matrix_hot = (block_matrix[:, None] == matrix_ids[None, :]).astype(F32)
    totals = jnp.sum(matrix_hot[:, :, None] * sums[:, None, :], axis=0)
    graft = jnp.sqrt(totals[:, 1]) / jnp.sqrt(totals[:, 0] + EPSILON)
    scales = jnp.sum(matrix_hot * graft[None, :], axis=1)

    place = me.reshape(1).astype(jnp.int32)
    update = scale_rows(0, local_total, scales, place, gathered, None)
    update = scale_rows(1, local_total, scales, place, gather_second(pieces_next), update)
    return (update.reshape(block_total, shard_rows, order), *stats)


def solution(mesh):
    return jax.shard_map(
        per_device,
        mesh=mesh,
        in_specs=(
            P(None, "dp", None),
            P("dp", "replica", None),
            P("dp", "replica", None),
            P("dp", "replica", None, None, None),
            P("dp", "replica", None, None, None),
            P(),
            P(),
            P(),
        ),
        out_specs=(P(None, "dp", None), P("dp", "replica", None), P("dp", "replica", None)),
        check_vma=False,
    )
```

```python
import jax
import jax.numpy as jnp
from jax import lax
from jax.experimental import pallas as pl
from jax.experimental.pallas import tpu as pltpu
from jax.sharding import PartitionSpec as P

NMAT = 5
STAT_DECAY = 0.95
EPSILON = 1e-06
BF16 = jnp.bfloat16
F32 = jnp.float32
EXTRA = 16
SUM_SCALE = 1.0 / 16.0


def params(steps=1, mib=60):
    semantics = ("arbitrary",) * steps if steps else None
    return pltpu.CompilerParams(dimension_semantics=semantics, vmem_limit_bytes=mib * 1024 * 1024)


def cost(flops, size):
    return pl.CostEstimate(flops=flops, bytes_accessed=size, transcendentals=0)


def shift(x, step):
    count = lax.axis_size("replica")
    return lax.ppermute(x, "replica", [(i, (i + step) % count) for i in range(count)])


def over_dp(x):
    return lax.all_to_all(x, "dp", split_axis=0, concat_axis=0, tiled=True)


def anywhere(count):
    return [pl.BlockSpec(memory_space=pl.ANY)] * count


SMEM = pl.BlockSpec(memory_space=pltpu.SMEM)


def pick_kernel(b, source, out, held, come, go):
    parts = come.shape[0]
    size = held.shape[0] // parts
    spans = [pl.ds(i * size, size) for i in range(parts)]
    reads = [
        pltpu.make_async_copy(source.at[span, b], held.at[span], come.at[i])
        for i, span in enumerate(spans)
    ]
    writes = [
        pltpu.make_async_copy(held.at[span], out.at[span], go.at[i]) for i, span in enumerate(spans)
    ]
    for read in reads:
        read.start()
    for read, write in zip(reads, writes):
        read.wait()
        write.start()
    for write in writes:
        write.wait()


def pick_block(by_owner, b, parts=8):
    count, _, rows, order = by_owner.shape
    return pl.pallas_call(
        lambda *refs: pick_kernel(b, *refs),
        out_shape=jax.ShapeDtypeStruct((count, rows, order), BF16),
        in_specs=anywhere(1),
        out_specs=anywhere(1)[0],
        scratch_shapes=[
            pltpu.VMEM((count, rows, order), BF16),
            pltpu.SemaphoreType.DMA((parts,)),
            pltpu.SemaphoreType.DMA((parts,)),
        ],
        compiler_params=params(0),
        cost_estimate=cost(0, 8 * count * rows * order),
        name="pick",
    )(by_owner)


def piece_places(me, pieces):
    count, _, width = pieces[0].shape
    for i, piece in enumerate(pieces):
        column = lax.rem(me + (0, 3, 1, 2, 2)[i], 4) * width
        first = count // 2 if i == 4 else 0
        yield piece, pl.ds(first, piece.shape[0]), pl.ds(pl.multiple_of(column, width), width)


def block_copies(me, pieces, block, sems):
    if len(pieces) == 1:
        return [pltpu.make_async_copy(pieces[0], block, sems.at[0])]
    return [
        pltpu.make_async_copy(piece, block.at[chunks, :, columns], sems.at[i])
        for i, (piece, chunks, columns) in enumerate(piece_places(me, pieces))
    ]


def sum_squares(x):
    wide = x.astype(F32)
    return jnp.sum(jnp.square(wide).reshape(-1, 8, wide.shape[-1]), axis=0)


def split_sum(total, first, rows, shape):
    value = jnp.full(shape, jnp.sum(total) * SUM_SCALE, F32)
    out = jnp.zeros(shape, F32)
    for part in range(3):
        rounded = value.astype(BF16).astype(F32)
        out = jnp.where(rows == first + part, rounded, out)
        value = jnp.where(value == rounded, 0.0, value - rounded)
    return out


def roots_kernel(parts, last, info, left, right, *refs):
    pieces, refs = refs[:parts], refs[parts:]
    if last:
        before, refs = refs[0], refs[1:]
    outs, (block, left_held, right_held, middle, pre_sum, grad_sum, sems) = refs[:-7], refs[-7:]
    to_right, to_left, keep_right, keep_left, own = outs[:5]
    slot, owned, me = info[0], info[1] == 1, info[2]
    order = middle.shape[0]
    wide = order // 2
    width = order // 4
    pre_sum[...] = jnp.zeros_like(pre_sum)
    grad_sum[...] = jnp.zeros_like(grad_sum)

    @pl.when(owned)
    def _():
        first = block_copies(me, pieces, block, sems)
        first.append(pltpu.make_async_copy(left.at[slot], left_held, sems.at[8]))
        second = []
        for place, offset in enumerate((2, 1, 3, 0)):
            column = pl.multiple_of(lax.rem(me + offset, 4) * width, width)
            source = right.at[slot, :, pl.ds(column, width)]
            target = right_held.at[:, pl.ds(place * width, width)]
            second.append(pltpu.make_async_copy(source, target, sems.at[9 + place]))
        for copy in first + second:
            copy.start()
        for copy in first:
            copy.wait()

        @pl.loop(0, 2)
        def _(i):
            columns = pl.ds(pl.multiple_of(i * wide, wide), wide)
            values = block[:, :, columns].reshape(order, wide)
            product = jnp.dot(left_held[...], values, preferred_element_type=F32)
            middle[:, columns] = product.astype(BF16)
            grad_sum[...] += sum_squares(values)

        for copy in second:
            copy.wait()
        for i in range(2):
            columns = slice(i * wide, (i + 1) * wide)
            product = jnp.dot(middle[...], right_held[:, columns], preferred_element_type=F32)
            product = product.astype(BF16)
            pre_sum[...] += sum_squares(product)
            chunks = product.reshape(block.shape[0], block.shape[1], wide)
            near, far = chunks[:, :, :width], chunks[:, :, width:]
            half = block.shape[0] // 2
            if i == 0:
                to_right[half : 2 * half] = near[:half]
                to_left[half : 2 * half] = near[half:]
                keep_right[:half] = far[:half]
                to_right[:half] = far[half:]
            else:
                to_left[:half] = near[:half]
                keep_left[:half] = near[half:]
                own[: 2 * half] = far

    shape = (block.shape[1], width)
    at = lax.broadcasted_iota(jnp.int32, shape, 0)
    extra = split_sum(pre_sum[...], 0, at, shape) + split_sum(grad_sum[...], 3, at, shape)
    if last:
        lane = lax.broadcasted_iota(jnp.int32, shape, 1)
        extra = jnp.where(lane < width // 2, before[...].astype(F32), extra).astype(BF16)
        for out in outs:
            out[out.shape[0] - 1] = extra
    else:
        outs[5][...] = extra.astype(BF16)


def apply_roots(info, left, pieces, right, before=None):
    order = left.shape[-1]
    width = order // 4
    rows = pieces[0].shape[-2]
    count = order // rows
    more = 0 if before is None else 1
    sizes = (count, count, count // 2, count // 2, count)
    shapes = [(size + more, rows, width) for size in sizes] + [(rows, width)] * (1 - more)
    operands = [info, left, right, *pieces]
    in_specs = [SMEM] + anywhere(len(operands) - 1)
    if before is not None:
        operands.append(before)
        in_specs.append(pl.BlockSpec(before.shape, lambda: (0, 0)))
    square = pltpu.VMEM((order, order), BF16)
    zeros = {2: lambda: (0, 0), 3: lambda: (0, 0, 0)}
    return pl.pallas_call(
        lambda *refs: roots_kernel(len(pieces), before is not None, *refs),
        out_shape=[jax.ShapeDtypeStruct(shape, BF16) for shape in shapes],
        in_specs=in_specs,
        out_specs=[pl.BlockSpec(shape, zeros[len(shape)]) for shape in shapes],
        scratch_shapes=[
            pltpu.VMEM((count, rows, order), BF16),
            square,
            square,
            square,
            pltpu.VMEM((8, order // 2), F32),
            pltpu.VMEM((8, order // 2), F32),
            pltpu.SemaphoreType.DMA((13,)),
        ],
        compiler_params=params(0, 50),
        cost_estimate=cost(16 * order**3, 10 * order * order),
        name="roots",
    )(*operands)


def stats_kernel(parts, info, *refs):
    pieces, (stat_left, stat_right), refs = refs[:parts], refs[parts : parts + 2], refs[parts + 2 :]
    new_left, new_right, block, turned, sems = refs[-5:]
    step = pl.program_id(0)
    width, order = turned.shape
    wide = new_left.shape[-1]
    rows = block.shape[1]
    start = pl.multiple_of(info[2] * width, width)
    span = width // rows

    @pl.when(step == 0)
    def _():
        copies = block_copies(info[2], pieces, block, sems)
        for copy in copies:
            copy.start()
        for copy in copies:
            copy.wait()
        turned[...] = block[:, :, pl.ds(start, width)].reshape(order, width).T

    mine = block[pl.ds(info[2] * span, span)].reshape(width, order)
    chunks = pl.ds(step * (wide // rows), wide // rows)
    others = block[chunks].reshape(wide, order)
    outer = lax.dot_general(mine, others, (((1,), (1,)), ((), ())), preferred_element_type=F32)
    new_left[0] = STAT_DECAY * stat_left[0] + (1.0 - STAT_DECAY) * outer
    columns = block[:, :, pl.ds(pl.multiple_of(step * wide, wide), wide)].reshape(order, wide)
    inner = jnp.dot(turned[...], columns, preferred_element_type=F32)
    new_right[0] = STAT_DECAY * stat_right[0] + (1.0 - STAT_DECAY) * inner


def update_stats(b, info, pieces, stat_left, stat_right, earlier, steps=2):
    _, rows, order = stat_left.shape
    spec = pl.BlockSpec((1, rows, order // steps), lambda step: (b, 0, step))
    operands = [info, *pieces, stat_left, stat_right]
    in_specs = [SMEM] + anywhere(len(pieces)) + [spec, spec]
    aliases = {}
    if earlier is not None:
        aliases = {len(operands): 0, len(operands) + 1: 1}
        operands += earlier
        in_specs += anywhere(2)
    chunk_rows = pieces[0].shape[-2]
    return pl.pallas_call(
        lambda *refs: stats_kernel(len(pieces), *refs),
        out_shape=[jax.ShapeDtypeStruct(stat_left.shape, F32)] * 2,
        grid=(steps,),
        in_specs=in_specs,
        out_specs=[spec, spec],
        scratch_shapes=[
            pltpu.VMEM((order // chunk_rows, chunk_rows, order), BF16),
            pltpu.VMEM((rows, order), BF16),
            pltpu.SemaphoreType.DMA((8,)),
        ],
        input_output_aliases=aliases,
        compiler_params=params(),
        cost_estimate=cost(24 * rows * order**2, 2 * order * order + 16 * rows * order),
        name="stats",
    )(*operands)


def scale_kernel(which, slots, parts, scales, place, *refs):
    pieces = refs[:parts]
    out, held, ready, come, go = refs[-5:]
    half = held.shape[1]
    reads = []
    for part in range(2):
        for at in range(4):
            i = 4 * part + at
            if parts == 8:
                source = pieces[i]
            else:
                source = pieces[3 + part] if at == 3 else pieces[at].at[pl.ds(part * half, half)]
            reads.append(pltpu.make_async_copy(source, held.at[i], come.at[i]))
    for read in reads:
        read.start()
    writes = []
    for part in range(2):
        for read in reads[4 * part : 4 * part + 4]:
            read.wait()
        for i in range(half):
            factor = scales[(part * half + i) * slots + which]
            for at, (_, _, columns) in enumerate(piece_places(place[0], pieces[:4])):
                values = held[4 * part + at, i].astype(F32) * factor
                ready[part * half + i, :, columns] = values.astype(BF16)
        span = pl.ds(part * half, half)
        writes.append(pltpu.make_async_copy(ready.at[span], out.at[span, which], go.at[part]))
        writes[-1].start()
    for write in writes:
        write.wait()


def scale_rows(which, slots, scales, place, pieces, earlier):
    count, rows, width = pieces[0].shape
    count = 2 * count if len(pieces) == 8 else count
    operands = [scales, place, *pieces] + ([] if earlier is None else [earlier])
    return pl.pallas_call(
        lambda *refs: scale_kernel(which, slots, len(pieces), *refs),
        out_shape=jax.ShapeDtypeStruct((count, slots, rows, 4 * width), BF16),
        in_specs=[SMEM, SMEM] + anywhere(len(operands) - 2),
        out_specs=anywhere(1)[0],
        scratch_shapes=[
            pltpu.VMEM((8, count // 2, rows, width), BF16),
            pltpu.VMEM((count, rows, 4 * width), BF16),
            pltpu.SemaphoreType.DMA((8,)),
            pltpu.SemaphoreType.DMA((2,)),
        ],
        input_output_aliases={} if earlier is None else {len(operands) - 1: 0},
        compiler_params=params(0, 50),
        cost_estimate=cost(0, 48 * count * rows * width),
        name="scale",
    )(*operands)


def in_order(first, *later):
    return lax.optimization_barrier((first, *later))


def scatter_first(messages):
    return shift(messages[0], 1), shift(messages[1], -1)


def choose_second(messages, first, mine):
    _, _, keep_right, keep_left, own = messages
    half = own.shape[0] // 2
    from_left, from_right = first
    return jnp.where(mine, keep_right, from_left[half:]), jnp.where(mine, keep_left, from_right[half:])


def scatter_second(chosen):
    return shift(chosen[0], 1), shift(chosen[1], -1)


def merge(messages, first, second, away):
    own, half = messages[4], messages[4].shape[0] // 2
    low = jnp.where(away == 1, first[1][:half], second[0][:half])
    low = jnp.where(away == 0, own[:half], low)
    high = jnp.where(away == 3, first[0][:half], second[1][:half])
    high = jnp.where(away == 0, own[half : 2 * half], high)
    return jnp.concatenate([low, high], axis=0)


def gather_first(quarter):
    return quarter, shift(quarter, 1), shift(quarter, -1)


def gather_halves(low, high):
    left_low = shift(low, 1)
    right_high = shift(high, -1)
    left_high = shift(high, 1)
    right_low = shift(low, -1)
    far_low = shift(left_low, 1)
    far_high = shift(right_high, -1)
    return [low, left_low, right_low, far_low, high, left_high, right_high, far_high]


def gather_second(pieces):
    _, left, right = pieces
    half = left.shape[0] // 2
    return [*pieces, shift(left[:half], 1), shift(right[half:], -1)]


def per_device(
    gradients, stat_left, stat_right, inv_left, inv_right, owned_blocks, owner_counts, block_matrix
):
    dp_count = lax.axis_size("dp")
    owner_total = lax.axis_size("replica")
    dp_index = lax.axis_index("dp")
    me = lax.axis_index("replica")
    block_total, shard_rows, order = gradients.shape
    local_total = block_total // dp_count
    slot_total = inv_left.shape[2]
    width = order // owner_total
    half = dp_count // 2

    by_owner = gradients.reshape(dp_count, local_total, shard_rows, order)
    my_columns = lax.dynamic_slice(
        by_owner, (0, 0, 0, me * width), (dp_count, 1, shard_rows, width)
    ).reshape(dp_count, shard_rows, width)
    first_pieces = gather_first(over_dp(my_columns))
    second_block = over_dp(pick_block(by_owner, 1))
    blocks = [gather_second(first_pieces), [second_block]]

    slot_ids = jnp.arange(slot_total, dtype=jnp.int32)
    live = slot_ids[None, None, :] < owner_counts[:, :, None]
    replica_ids = jnp.arange(owner_total, dtype=jnp.int32)
    infos, owners = [], []
    for b in range(local_total):
        match = (owned_blocks == b) & live
        owners.append(jnp.sum(jnp.where(match, replica_ids[None, :, None], 0), axis=(1, 2)))
        slots = jnp.sum(jnp.where(match, slot_ids[None, None, :], 0), axis=(1, 2))
        owner = lax.dynamic_index_in_dim(owners[b], dp_index, 0, keepdims=False)
        slot = lax.dynamic_index_in_dim(slots, dp_index, 0, keepdims=False)
        away = lax.rem(owner - me + owner_total, owner_total)
        info = jnp.stack([slot, (away == 0).astype(jnp.int32), me, away])
        infos.append(info.astype(jnp.int32))

    away = [info[3] for info in infos]

    *sent, sums = apply_roots(infos[0], inv_left[0, 0], blocks[0], inv_right[0, 0])
    got = scatter_first(sent)
    sent_next = apply_roots(infos[1], inv_left[0, 0], blocks[1], inv_right[0, 0], sums)
    sent_next, got = in_order(sent_next, got)
    got_more = scatter_second(choose_second(sent, got, away[0] == 0))
    got_next = scatter_first(sent_next)
    first = over_dp(merge(sent, got, got_more, away[0]))

    chunk = lax.broadcasted_iota(jnp.int32, sent_next[2].shape, 0)
    lane = lax.broadcasted_iota(jnp.int32, sent_next[2].shape, 2)
    of_before = (chunk == half) & (lane < width // 2)
    mine = jnp.where(of_before, away[0], away[1]) == 0
    got_next_more = scatter_second(choose_second(sent_next, got_next, mine))
    far_off = jnp.where(of_before[half], away[0], away[1])
    sums = jnp.where(far_off == 1, got_next[1][2 * half], got_next_more[0][half])
    sums = jnp.where(far_off == 3, got_next[0][2 * half], sums)
    sums = jnp.where(far_off == 0, sent_next[4][2 * half], sums)
    sums = jnp.broadcast_to(sums[None, :EXTRA], (dp_count, EXTRA, width))
    quarter = merge(sent_next, got_next, got_next_more, away[1])
    second = over_dp(jnp.concatenate([quarter, sums], axis=1))

    pieces = gather_first(first)
    pieces, stat_left, stat_right = in_order(pieces, stat_left, stat_right)
    stats = update_stats(0, infos[0], blocks[0], stat_left, stat_right, None)
    second, stats = in_order(second, stats)
    stats = update_stats(1, infos[1], blocks[1], stat_left, stat_right, stats)
    gathered = gather_second(pieces)
    pieces_next = gather_halves(second[:half, :shard_rows], second[half:, :shard_rows])
    sums = second[:, shard_rows : shard_rows + 6, :].astype(F32)
    sums = sums.reshape(dp_count, 2, 3, local_total, width // local_total)[..., 0]
    sums = jnp.sum(sums, axis=2) / SUM_SCALE
    sums = jnp.swapaxes(sums, 1, 2).reshape(block_total, 2)

    matrix_ids = jnp.arange(NMAT, dtype=jnp.int32)
    matrix_hot = (block_matrix[:, None] == matrix_ids[None, :]).astype(F32)
    totals = jnp.sum(matrix_hot[:, :, None] * sums[:, None, :], axis=0)
    graft = jnp.sqrt(totals[:, 1]) / jnp.sqrt(totals[:, 0] + EPSILON)
    scales = jnp.sum(matrix_hot * graft[None, :], axis=1)

    place = me.reshape(1).astype(jnp.int32)
    update = scale_rows(0, local_total, scales, place, gathered, None)
    update = scale_rows(1, local_total, scales, place, pieces_next, update)
    return (update.reshape(block_total, shard_rows, order), *stats)


def solution(mesh):
    return jax.shard_map(
        per_device,
        mesh=mesh,
        in_specs=(
            P(None, "dp", None),
            P("dp", "replica", None),
            P("dp", "replica", None),
            P("dp", "replica", None, None, None),
            P("dp", "replica", None, None, None),
            P(),
            P(),
            P(),
        ),
        out_specs=(P(None, "dp", None), P("dp", "replica", None), P("dp", "replica", None)),
        check_vma=False,
    )
```

```python
import jax
import jax.numpy as jnp
from jax import lax
from jax.experimental import pallas as pl
from jax.experimental.pallas import tpu as pltpu
from jax.sharding import PartitionSpec as P

NMAT = 5
STAT_DECAY = 0.95
EPSILON = 1e-06
BF16 = jnp.bfloat16
F32 = jnp.float32
EXTRA = 16
SUM_SCALE = 1.0 / 16.0


def params(steps=1, mib=60):
    semantics = ("arbitrary",) * steps if steps else None
    return pltpu.CompilerParams(dimension_semantics=semantics, vmem_limit_bytes=mib * 1024 * 1024)


def cost(flops, size):
    return pl.CostEstimate(flops=flops, bytes_accessed=size, transcendentals=0)


def shift(x, step):
    count = lax.axis_size("replica")
    return lax.ppermute(x, "replica", [(i, (i + step) % count) for i in range(count)])


def over_dp(x):
    return lax.all_to_all(x, "dp", split_axis=0, concat_axis=0, tiled=True)


def anywhere(count):
    return [pl.BlockSpec(memory_space=pl.ANY)] * count


SMEM = pl.BlockSpec(memory_space=pltpu.SMEM)


def pick_kernel(b, source, out, held, come, go):
    parts = come.shape[0]
    size = held.shape[0] // parts
    spans = [pl.ds(i * size, size) for i in range(parts)]
    reads = [
        pltpu.make_async_copy(source.at[span, b], held.at[span], come.at[i])
        for i, span in enumerate(spans)
    ]
    writes = [
        pltpu.make_async_copy(held.at[span], out.at[span], go.at[i]) for i, span in enumerate(spans)
    ]
    for read in reads:
        read.start()
    for read, write in zip(reads, writes):
        read.wait()
        write.start()
    for write in writes:
        write.wait()


def pick_block(by_owner, b, parts=8):
    count, _, rows, order = by_owner.shape
    return pl.pallas_call(
        lambda *refs: pick_kernel(b, *refs),
        out_shape=jax.ShapeDtypeStruct((count, rows, order), BF16),
        in_specs=anywhere(1),
        out_specs=anywhere(1)[0],
        scratch_shapes=[
            pltpu.VMEM((count, rows, order), BF16),
            pltpu.SemaphoreType.DMA((parts,)),
            pltpu.SemaphoreType.DMA((parts,)),
        ],
        compiler_params=params(0),
        cost_estimate=cost(0, 8 * count * rows * order),
        name="pick",
    )(by_owner)


def piece_places(me, pieces):
    count, _, width = pieces[0].shape
    for i, piece in enumerate(pieces):
        column = lax.rem(me + (0, 3, 1, 2, 2)[i], 4) * width
        first = count // 2 if i == 4 else 0
        yield piece, pl.ds(first, piece.shape[0]), pl.ds(pl.multiple_of(column, width), width)


def block_copies(me, pieces, block, sems):
    if len(pieces) == 1:
        return [pltpu.make_async_copy(pieces[0], block, sems.at[0])]
    return [
        pltpu.make_async_copy(piece, block.at[chunks, :, columns], sems.at[i])
        for i, (piece, chunks, columns) in enumerate(piece_places(me, pieces))
    ]


def sum_squares(x):
    wide = x.astype(F32)
    return jnp.sum(jnp.square(wide).reshape(-1, 8, wide.shape[-1]), axis=0)


def split_sum(total, first, rows, shape):
    value = jnp.full(shape, jnp.sum(total) * SUM_SCALE, F32)
    out = jnp.zeros(shape, F32)
    for part in range(3):
        rounded = value.astype(BF16).astype(F32)
        out = jnp.where(rows == first + part, rounded, out)
        value = jnp.where(value == rounded, 0.0, value - rounded)
    return out


def roots_kernel(parts, last, info, left, right, *refs):
    pieces, refs = refs[:parts], refs[parts:]
    if last:
        before, refs = refs[0], refs[1:]
    outs, (block, left_held, right_held, middle, pre_sum, grad_sum, sems) = refs[:-7], refs[-7:]
    to_right, to_left, keep_right, keep_left, own = outs[:5]
    slot, owned, me = info[0], info[1] == 1, info[2]
    order = middle.shape[0]
    wide = order // 2
    width = order // 4
    pre_sum[...] = jnp.zeros_like(pre_sum)
    grad_sum[...] = jnp.zeros_like(grad_sum)

    @pl.when(owned)
    def _():
        first = block_copies(me, pieces, block, sems)
        tops = [pl.ds(i * wide, wide) for i in range(2)]
        halves = [
            pltpu.make_async_copy(left.at[slot, span], left_held.at[span], sems.at[7 + i])
            for i, span in enumerate(tops)
        ]
        second = []
        for place, offset in enumerate((2, 1, 3, 0)):
            column = pl.multiple_of(lax.rem(me + offset, 4) * width, width)
            source = right.at[slot, :, pl.ds(column, width)]
            target = right_held.at[:, pl.ds(place * width, width)]
            second.append(pltpu.make_async_copy(source, target, sems.at[9 + place]))
        for copy in first + halves:
            copy.start()
        for copy in first:
            copy.wait()
        for i, span in enumerate(tops):
            halves[i].wait()
            if i == 0:
                for copy in second:
                    copy.start()
            values = block[...].reshape(order, order)
            product = jnp.dot(left_held[span, :], values, preferred_element_type=F32)
            middle[span, :] = product.astype(BF16)
            squares = sum_squares(values[i * wide : (i + 1) * wide])
            grad_sum[...] += squares[:, :wide] + squares[:, wide:]

        for copy in second:
            copy.wait()
        for i in range(2):
            columns = slice(i * wide, (i + 1) * wide)
            product = jnp.dot(middle[...], right_held[:, columns], preferred_element_type=F32)
            product = product.astype(BF16)
            pre_sum[...] += sum_squares(product)
            chunks = product.reshape(block.shape[0], block.shape[1], wide)
            near, far = chunks[:, :, :width], chunks[:, :, width:]
            half = block.shape[0] // 2
            if i == 0:
                to_right[half : 2 * half] = near[:half]
                to_left[half : 2 * half] = near[half:]
                keep_right[:half] = far[:half]
                to_right[:half] = far[half:]
            else:
                to_left[:half] = near[:half]
                keep_left[:half] = near[half:]
                own[: 2 * half] = far

    shape = (block.shape[1], width)
    at = lax.broadcasted_iota(jnp.int32, shape, 0)
    extra = split_sum(pre_sum[...], 0, at, shape) + split_sum(grad_sum[...], 3, at, shape)
    if last:
        lane = lax.broadcasted_iota(jnp.int32, shape, 1)
        extra = jnp.where(lane < width // 2, before[...].astype(F32), extra).astype(BF16)
        for out in outs:
            out[out.shape[0] - 1] = extra
    else:
        outs[5][...] = extra.astype(BF16)


def apply_roots(info, left, pieces, right, before=None):
    order = left.shape[-1]
    width = order // 4
    rows = pieces[0].shape[-2]
    count = order // rows
    more = 0 if before is None else 1
    sizes = (count, count, count // 2, count // 2, count)
    shapes = [(size + more, rows, width) for size in sizes] + [(rows, width)] * (1 - more)
    operands = [info, left, right, *pieces]
    in_specs = [SMEM] + anywhere(len(operands) - 1)
    if before is not None:
        operands.append(before)
        in_specs.append(pl.BlockSpec(before.shape, lambda: (0, 0)))
    square = pltpu.VMEM((order, order), BF16)
    zeros = {2: lambda: (0, 0), 3: lambda: (0, 0, 0)}
    return pl.pallas_call(
        lambda *refs: roots_kernel(len(pieces), before is not None, *refs),
        out_shape=[jax.ShapeDtypeStruct(shape, BF16) for shape in shapes],
        in_specs=in_specs,
        out_specs=[pl.BlockSpec(shape, zeros[len(shape)]) for shape in shapes],
        scratch_shapes=[
            pltpu.VMEM((count, rows, order), BF16),
            square,
            square,
            square,
            pltpu.VMEM((8, order // 2), F32),
            pltpu.VMEM((8, order // 2), F32),
            pltpu.SemaphoreType.DMA((13,)),
        ],
        compiler_params=params(0, 50),
        cost_estimate=cost(16 * order**3, 10 * order * order),
        name="roots",
    )(*operands)


def stats_kernel(parts, info, *refs):
    pieces, (stat_left, stat_right), refs = refs[:parts], refs[parts : parts + 2], refs[parts + 2 :]
    new_left, new_right, block, turned, sems = refs[-5:]
    step = pl.program_id(0)
    width, order = turned.shape
    wide = new_left.shape[-1]
    rows = block.shape[1]
    start = pl.multiple_of(info[2] * width, width)
    span = width // rows

    @pl.when(step == 0)
    def _():
        copies = block_copies(info[2], pieces, block, sems)
        for copy in copies:
            copy.start()
        for copy in copies:
            copy.wait()
        turned[...] = block[:, :, pl.ds(start, width)].reshape(order, width).T

    mine = block[pl.ds(info[2] * span, span)].reshape(width, order)
    chunks = pl.ds(step * (wide // rows), wide // rows)
    others = block[chunks].reshape(wide, order)
    outer = lax.dot_general(mine, others, (((1,), (1,)), ((), ())), preferred_element_type=F32)
    new_left[0] = STAT_DECAY * stat_left[0] + (1.0 - STAT_DECAY) * outer
    columns = block[:, :, pl.ds(pl.multiple_of(step * wide, wide), wide)].reshape(order, wide)
    inner = jnp.dot(turned[...], columns, preferred_element_type=F32)
    new_right[0] = STAT_DECAY * stat_right[0] + (1.0 - STAT_DECAY) * inner


def update_stats(b, info, pieces, stat_left, stat_right, earlier, steps=2):
    _, rows, order = stat_left.shape
    spec = pl.BlockSpec((1, rows, order // steps), lambda step: (b, 0, step))
    operands = [info, *pieces, stat_left, stat_right]
    in_specs = [SMEM] + anywhere(len(pieces)) + [spec, spec]
    aliases = {}
    if earlier is not None:
        aliases = {len(operands): 0, len(operands) + 1: 1}
        operands += earlier
        in_specs += anywhere(2)
    chunk_rows = pieces[0].shape[-2]
    return pl.pallas_call(
        lambda *refs: stats_kernel(len(pieces), *refs),
        out_shape=[jax.ShapeDtypeStruct(stat_left.shape, F32)] * 2,
        grid=(steps,),
        in_specs=in_specs,
        out_specs=[spec, spec],
        scratch_shapes=[
            pltpu.VMEM((order // chunk_rows, chunk_rows, order), BF16),
            pltpu.VMEM((rows, order), BF16),
            pltpu.SemaphoreType.DMA((8,)),
        ],
        input_output_aliases=aliases,
        compiler_params=params(),
        cost_estimate=cost(24 * rows * order**2, 2 * order * order + 16 * rows * order),
        name="stats",
    )(*operands)


def scale_kernel(which, slots, parts, scales, place, *refs):
    pieces = refs[:parts]
    out, held, ready, come, go = refs[-5:]
    half = held.shape[1]
    reads = []
    for part in range(2):
        for at in range(4):
            i = 4 * part + at
            if parts == 8:
                source = pieces[i]
            else:
                source = pieces[3 + part] if at == 3 else pieces[at].at[pl.ds(part * half, half)]
            reads.append(pltpu.make_async_copy(source, held.at[i], come.at[i]))
    for read in reads:
        read.start()
    writes = []
    for part in range(2):
        for read in reads[4 * part : 4 * part + 4]:
            read.wait()
        for i in range(half):
            factor = scales[(part * half + i) * slots + which]
            for at, (_, _, columns) in enumerate(piece_places(place[0], pieces[:4])):
                values = held[4 * part + at, i].astype(F32) * factor
                ready[part * half + i, :, columns] = values.astype(BF16)
        span = pl.ds(part * half, half)
        writes.append(pltpu.make_async_copy(ready.at[span], out.at[span, which], go.at[part]))
        writes[-1].start()
    for write in writes:
        write.wait()


def scale_rows(which, slots, scales, place, pieces, earlier):
    count, rows, width = pieces[0].shape
    count = 2 * count if len(pieces) == 8 else count
    operands = [scales, place, *pieces] + ([] if earlier is None else [earlier])
    return pl.pallas_call(
        lambda *refs: scale_kernel(which, slots, len(pieces), *refs),
        out_shape=jax.ShapeDtypeStruct((count, slots, rows, 4 * width), BF16),
        in_specs=[SMEM, SMEM] + anywhere(len(operands) - 2),
        out_specs=anywhere(1)[0],
        scratch_shapes=[
            pltpu.VMEM((8, count // 2, rows, width), BF16),
            pltpu.VMEM((count, rows, 4 * width), BF16),
            pltpu.SemaphoreType.DMA((8,)),
            pltpu.SemaphoreType.DMA((2,)),
        ],
        input_output_aliases={} if earlier is None else {len(operands) - 1: 0},
        compiler_params=params(0, 50),
        cost_estimate=cost(0, 48 * count * rows * width),
        name="scale",
    )(*operands)


def in_order(first, *later):
    return lax.optimization_barrier((first, *later))


def scatter_first(messages):
    return shift(messages[0], 1), shift(messages[1], -1)


def choose_second(messages, first, mine):
    _, _, keep_right, keep_left, own = messages
    half = own.shape[0] // 2
    from_left, from_right = first
    return jnp.where(mine, keep_right, from_left[half:]), jnp.where(mine, keep_left, from_right[half:])


def scatter_second(chosen):
    return shift(chosen[0], 1), shift(chosen[1], -1)


def merge(messages, first, second, away):
    own, half = messages[4], messages[4].shape[0] // 2
    low = jnp.where(away == 1, first[1][:half], second[0][:half])
    low = jnp.where(away == 0, own[:half], low)
    high = jnp.where(away == 3, first[0][:half], second[1][:half])
    high = jnp.where(away == 0, own[half : 2 * half], high)
    return jnp.concatenate([low, high], axis=0)


def gather_first(quarter):
    return quarter, shift(quarter, 1), shift(quarter, -1)


def gather_halves(low, high):
    left_low = shift(low, 1)
    right_high = shift(high, -1)
    left_high = shift(high, 1)
    right_low = shift(low, -1)
    far_low = shift(left_low, 1)
    far_high = shift(right_high, -1)
    return [low, left_low, right_low, far_low, high, left_high, right_high, far_high]


def gather_second(pieces):
    _, left, right = pieces
    half = left.shape[0] // 2
    return [*pieces, shift(left[:half], 1), shift(right[half:], -1)]


def per_device(
    gradients, stat_left, stat_right, inv_left, inv_right, owned_blocks, owner_counts, block_matrix
):
    dp_count = lax.axis_size("dp")
    owner_total = lax.axis_size("replica")
    dp_index = lax.axis_index("dp")
    me = lax.axis_index("replica")
    block_total, shard_rows, order = gradients.shape
    local_total = block_total // dp_count
    slot_total = inv_left.shape[2]
    width = order // owner_total
    half = dp_count // 2

    by_owner = gradients.reshape(dp_count, local_total, shard_rows, order)
    my_columns = lax.dynamic_slice(
        by_owner, (0, 0, 0, me * width), (dp_count, 1, shard_rows, width)
    ).reshape(dp_count, shard_rows, width)
    first_pieces = gather_first(over_dp(my_columns))
    second_block = over_dp(pick_block(by_owner, 1))
    blocks = [gather_second(first_pieces), [second_block]]

    slot_ids = jnp.arange(slot_total, dtype=jnp.int32)
    live = slot_ids[None, None, :] < owner_counts[:, :, None]
    replica_ids = jnp.arange(owner_total, dtype=jnp.int32)
    infos, owners = [], []
    for b in range(local_total):
        match = (owned_blocks == b) & live
        owners.append(jnp.sum(jnp.where(match, replica_ids[None, :, None], 0), axis=(1, 2)))
        slots = jnp.sum(jnp.where(match, slot_ids[None, None, :], 0), axis=(1, 2))
        owner = lax.dynamic_index_in_dim(owners[b], dp_index, 0, keepdims=False)
        slot = lax.dynamic_index_in_dim(slots, dp_index, 0, keepdims=False)
        away = lax.rem(owner - me + owner_total, owner_total)
        info = jnp.stack([slot, (away == 0).astype(jnp.int32), me, away])
        infos.append(info.astype(jnp.int32))

    away = [info[3] for info in infos]

    *sent, sums = apply_roots(infos[0], inv_left[0, 0], blocks[0], inv_right[0, 0])
    got = scatter_first(sent)
    sent_next = apply_roots(infos[1], inv_left[0, 0], blocks[1], inv_right[0, 0], sums)
    sent_next, got = in_order(sent_next, got)
    got_more = scatter_second(choose_second(sent, got, away[0] == 0))
    got_next = scatter_first(sent_next)
    first = over_dp(merge(sent, got, got_more, away[0]))

    chunk = lax.broadcasted_iota(jnp.int32, sent_next[2].shape, 0)
    lane = lax.broadcasted_iota(jnp.int32, sent_next[2].shape, 2)
    of_before = (chunk == half) & (lane < width // 2)
    mine = jnp.where(of_before, away[0], away[1]) == 0
    got_next_more = scatter_second(choose_second(sent_next, got_next, mine))
    far_off = jnp.where(of_before[half], away[0], away[1])
    sums = jnp.where(far_off == 1, got_next[1][2 * half], got_next_more[0][half])
    sums = jnp.where(far_off == 3, got_next[0][2 * half], sums)
    sums = jnp.where(far_off == 0, sent_next[4][2 * half], sums)
    sums = jnp.broadcast_to(sums[None, :EXTRA], (dp_count, EXTRA, width))
    quarter = merge(sent_next, got_next, got_next_more, away[1])
    second = over_dp(jnp.concatenate([quarter, sums], axis=1))

    pieces = gather_first(first)
    pieces, stat_left, stat_right = in_order(pieces, stat_left, stat_right)
    stats = update_stats(0, infos[0], blocks[0], stat_left, stat_right, None)
    second, stats = in_order(second, stats)
    stats = update_stats(1, infos[1], blocks[1], stat_left, stat_right, stats)
    gathered = gather_second(pieces)
    pieces_next = gather_halves(second[:half, :shard_rows], second[half:, :shard_rows])
    sums = second[:, shard_rows : shard_rows + 6, :].astype(F32)
    sums = sums.reshape(dp_count, 2, 3, local_total, width // local_total)[..., 0]
    sums = jnp.sum(sums, axis=2) / SUM_SCALE
    sums = jnp.swapaxes(sums, 1, 2).reshape(block_total, 2)

    matrix_ids = jnp.arange(NMAT, dtype=jnp.int32)
    matrix_hot = (block_matrix[:, None] == matrix_ids[None, :]).astype(F32)
    totals = jnp.sum(matrix_hot[:, :, None] * sums[:, None, :], axis=0)
    graft = jnp.sqrt(totals[:, 1]) / jnp.sqrt(totals[:, 0] + EPSILON)
    scales = jnp.sum(matrix_hot * graft[None, :], axis=1)

    place = me.reshape(1).astype(jnp.int32)
    update = scale_rows(0, local_total, scales, place, gathered, None)
    update = scale_rows(1, local_total, scales, place, pieces_next, update)
    return (update.reshape(block_total, shard_rows, order), *stats)


def solution(mesh):
    return jax.shard_map(
        per_device,
        mesh=mesh,
        in_specs=(
            P(None, "dp", None),
            P("dp", "replica", None),
            P("dp", "replica", None),
            P("dp", "replica", None, None, None),
            P("dp", "replica", None, None, None),
            P(),
            P(),
            P(),
        ),
        out_specs=(P(None, "dp", None), P("dp", "replica", None), P("dp", "replica", None)),
        check_vma=False,
    )
```

```python
import jax
import jax.numpy as jnp
from jax import lax
from jax.experimental import pallas as pl
from jax.experimental.pallas import tpu as pltpu
from jax.sharding import PartitionSpec as P

NMAT = 5
STAT_DECAY = 0.95
EPSILON = 1e-06
BF16 = jnp.bfloat16
F32 = jnp.float32
EXTRA = 16
SUM_SCALE = 1.0 / 16.0


def params(steps=1, mib=60):
    semantics = ("arbitrary",) * steps if steps else None
    return pltpu.CompilerParams(dimension_semantics=semantics, vmem_limit_bytes=mib * 1024 * 1024)


def cost(flops, size):
    return pl.CostEstimate(flops=flops, bytes_accessed=size, transcendentals=0)


def shift(x, step):
    count = lax.axis_size("replica")
    return lax.ppermute(x, "replica", [(i, (i + step) % count) for i in range(count)])


def over_dp(x):
    return lax.all_to_all(x, "dp", split_axis=0, concat_axis=0, tiled=True)


def anywhere(count):
    return [pl.BlockSpec(memory_space=pl.ANY)] * count


SMEM = pl.BlockSpec(memory_space=pltpu.SMEM)


def pick_kernel(b, source, out, held, come, go):
    parts = come.shape[0]
    size = held.shape[0] // parts
    spans = [pl.ds(i * size, size) for i in range(parts)]
    reads = [
        pltpu.make_async_copy(source.at[span, b], held.at[span], come.at[i])
        for i, span in enumerate(spans)
    ]
    writes = [
        pltpu.make_async_copy(held.at[span], out.at[span], go.at[i]) for i, span in enumerate(spans)
    ]
    for read in reads:
        read.start()
    for read, write in zip(reads, writes):
        read.wait()
        write.start()
    for write in writes:
        write.wait()


def pick_block(by_owner, b, parts=8):
    count, _, rows, order = by_owner.shape
    return pl.pallas_call(
        lambda *refs: pick_kernel(b, *refs),
        out_shape=jax.ShapeDtypeStruct((count, rows, order), BF16),
        in_specs=anywhere(1),
        out_specs=anywhere(1)[0],
        scratch_shapes=[
            pltpu.VMEM((count, rows, order), BF16),
            pltpu.SemaphoreType.DMA((parts,)),
            pltpu.SemaphoreType.DMA((parts,)),
        ],
        compiler_params=params(0, 50),
        cost_estimate=cost(0, 8 * count * rows * order),
        name="pick",
    )(by_owner)


def piece_places(me, pieces):
    count, _, width = pieces[0].shape
    for i, piece in enumerate(pieces):
        column = lax.rem(me + (0, 3, 1, 2, 2)[i], 4) * width
        first = count // 2 if i == 4 else 0
        yield piece, pl.ds(first, piece.shape[0]), pl.ds(pl.multiple_of(column, width), width)


def block_copies(me, pieces, block, sems):
    if len(pieces) == 1:
        return [pltpu.make_async_copy(pieces[0], block, sems.at[0])]
    return [
        pltpu.make_async_copy(piece, block.at[chunks, :, columns], sems.at[i])
        for i, (piece, chunks, columns) in enumerate(piece_places(me, pieces))
    ]


def sum_squares(x):
    wide = x.astype(F32)
    return jnp.sum(jnp.square(wide).reshape(-1, 8, wide.shape[-1]), axis=0)


def split_sum(total, first, rows, shape):
    value = jnp.full(shape, jnp.sum(total) * SUM_SCALE, F32)
    out = jnp.zeros(shape, F32)
    for part in range(3):
        rounded = value.astype(BF16).astype(F32)
        out = jnp.where(rows == first + part, rounded, out)
        value = jnp.where(value == rounded, 0.0, value - rounded)
    return out


def roots_kernel(parts, last, info, left, right, *refs):
    pieces, refs = refs[:parts], refs[parts:]
    if last:
        before, refs = refs[0], refs[1:]
    outs, (block, left_held, right_held, middle, pre_sum, grad_sum, sems) = refs[:-7], refs[-7:]
    to_right, to_left, keep_right, keep_left, own = outs[:5]
    slot, owned, me = info[0], info[1] == 1, info[2]
    order = middle.shape[0]
    wide = order // 2
    width = order // 4
    pre_sum[...] = jnp.zeros_like(pre_sum)
    grad_sum[...] = jnp.zeros_like(grad_sum)

    @pl.when(owned)
    def _():
        first = block_copies(me, pieces, block, sems)
        tops = [pl.ds(i * wide, wide) for i in range(2)]
        halves = [
            pltpu.make_async_copy(left.at[slot, span], left_held.at[span], sems.at[7 + i])
            for i, span in enumerate(tops)
        ]
        second = []
        for place, offset in enumerate((2, 1, 3, 0)):
            column = pl.multiple_of(lax.rem(me + offset, 4) * width, width)
            source = right.at[slot, :, pl.ds(column, width)]
            target = right_held.at[:, pl.ds(place * width, width)]
            second.append(pltpu.make_async_copy(source, target, sems.at[9 + place]))
        for copy in first + halves:
            copy.start()
        for copy in first:
            copy.wait()
        for i, span in enumerate(tops):
            halves[i].wait()
            if i == 0:
                for copy in second:
                    copy.start()
            values = block[...].reshape(order, order)
            product = jnp.dot(left_held[span, :], values, preferred_element_type=F32)
            middle[span, :] = product.astype(BF16)
            squares = sum_squares(values[i * wide : (i + 1) * wide])
            grad_sum[...] += squares[:, :wide] + squares[:, wide:]

        for copy in second:
            copy.wait()
        for i in range(2):
            columns = slice(i * wide, (i + 1) * wide)
            product = jnp.dot(middle[...], right_held[:, columns], preferred_element_type=F32)
            product = product.astype(BF16)
            pre_sum[...] += sum_squares(product)
            chunks = product.reshape(block.shape[0], block.shape[1], wide)
            near, far = chunks[:, :, :width], chunks[:, :, width:]
            half = block.shape[0] // 2
            if i == 0:
                to_right[half : 2 * half] = near[:half]
                to_left[half : 2 * half] = near[half:]
                keep_right[:half] = far[:half]
                to_right[:half] = far[half:]
            else:
                to_left[:half] = near[:half]
                keep_left[:half] = near[half:]
                own[: 2 * half] = far

    shape = (block.shape[1], width)
    at = lax.broadcasted_iota(jnp.int32, shape, 0)
    extra = split_sum(pre_sum[...], 0, at, shape) + split_sum(grad_sum[...], 3, at, shape)
    if last:
        lane = lax.broadcasted_iota(jnp.int32, shape, 1)
        extra = jnp.where(lane < width // 2, before[...].astype(F32), extra).astype(BF16)
        for out in outs:
            out[out.shape[0] - 1] = extra
    else:
        outs[5][...] = extra.astype(BF16)


def apply_roots(info, left, pieces, right, before=None):
    order = left.shape[-1]
    width = order // 4
    rows = pieces[0].shape[-2]
    count = order // rows
    more = 0 if before is None else 1
    sizes = (count, count, count // 2, count // 2, count)
    shapes = [(size + more, rows, width) for size in sizes] + [(rows, width)] * (1 - more)
    operands = [info, left, right, *pieces]
    in_specs = [SMEM] + anywhere(len(operands) - 1)
    if before is not None:
        operands.append(before)
        in_specs.append(pl.BlockSpec(before.shape, lambda: (0, 0)))
    square = pltpu.VMEM((order, order), BF16)
    zeros = {2: lambda: (0, 0), 3: lambda: (0, 0, 0)}
    return pl.pallas_call(
        lambda *refs: roots_kernel(len(pieces), before is not None, *refs),
        out_shape=[jax.ShapeDtypeStruct(shape, BF16) for shape in shapes],
        in_specs=in_specs,
        out_specs=[pl.BlockSpec(shape, zeros[len(shape)]) for shape in shapes],
        scratch_shapes=[
            pltpu.VMEM((count, rows, order), BF16),
            square,
            square,
            square,
            pltpu.VMEM((8, order // 2), F32),
            pltpu.VMEM((8, order // 2), F32),
            pltpu.SemaphoreType.DMA((13,)),
        ],
        compiler_params=params(0, 50),
        cost_estimate=cost(16 * order**3, 10 * order * order),
        name="roots",
    )(*operands)


def stats_kernel(parts, info, *refs):
    pieces, (stat_left, stat_right), refs = refs[:parts], refs[parts : parts + 2], refs[parts + 2 :]
    new_left, new_right, block, turned, sems = refs[-5:]
    step = pl.program_id(0)
    width, order = turned.shape
    wide = new_left.shape[-1]
    rows = block.shape[1]
    start = pl.multiple_of(info[2] * width, width)
    span = width // rows

    @pl.when(step == 0)
    def _():
        copies = block_copies(info[2], pieces, block, sems)
        for copy in copies:
            copy.start()
        for copy in copies:
            copy.wait()
        turned[...] = block[:, :, pl.ds(start, width)].reshape(order, width).T

    mine = block[pl.ds(info[2] * span, span)].reshape(width, order)
    chunks = pl.ds(step * (wide // rows), wide // rows)
    others = block[chunks].reshape(wide, order)
    outer = lax.dot_general(mine, others, (((1,), (1,)), ((), ())), preferred_element_type=F32)
    new_left[0] = STAT_DECAY * stat_left[0] + (1.0 - STAT_DECAY) * outer
    columns = block[:, :, pl.ds(pl.multiple_of(step * wide, wide), wide)].reshape(order, wide)
    inner = jnp.dot(turned[...], columns, preferred_element_type=F32)
    new_right[0] = STAT_DECAY * stat_right[0] + (1.0 - STAT_DECAY) * inner


def update_stats(b, info, pieces, stat_left, stat_right, earlier, steps=2):
    _, rows, order = stat_left.shape
    spec = pl.BlockSpec((1, rows, order // steps), lambda step: (b, 0, step))
    operands = [info, *pieces, stat_left, stat_right]
    in_specs = [SMEM] + anywhere(len(pieces)) + [spec, spec]
    aliases = {}
    if earlier is not None:
        aliases = {len(operands): 0, len(operands) + 1: 1}
        operands += earlier
        in_specs += anywhere(2)
    chunk_rows = pieces[0].shape[-2]
    return pl.pallas_call(
        lambda *refs: stats_kernel(len(pieces), *refs),
        out_shape=[jax.ShapeDtypeStruct(stat_left.shape, F32)] * 2,
        grid=(steps,),
        in_specs=in_specs,
        out_specs=[spec, spec],
        scratch_shapes=[
            pltpu.VMEM((order // chunk_rows, chunk_rows, order), BF16),
            pltpu.VMEM((rows, order), BF16),
            pltpu.SemaphoreType.DMA((8,)),
        ],
        input_output_aliases=aliases,
        compiler_params=params(),
        cost_estimate=cost(24 * rows * order**2, 2 * order * order + 16 * rows * order),
        name="stats",
    )(*operands)


def scale_kernel(which, slots, parts, scales, place, *refs):
    pieces = refs[:parts]
    out, held, ready, come, go = refs[-5:]
    half = held.shape[1]
    reads = []
    for part in range(2):
        for at in range(4):
            i = 4 * part + at
            if parts == 8:
                source = pieces[i]
            else:
                source = pieces[3 + part] if at == 3 else pieces[at].at[pl.ds(part * half, half)]
            reads.append(pltpu.make_async_copy(source, held.at[i], come.at[i]))
    for read in reads:
        read.start()
    writes = []
    for part in range(2):
        for read in reads[4 * part : 4 * part + 4]:
            read.wait()
        for i in range(half):
            factor = scales[(part * half + i) * slots + which]
            for at, (_, _, columns) in enumerate(piece_places(place[0], pieces[:4])):
                values = held[4 * part + at, i].astype(F32) * factor
                ready[part * half + i, :, columns] = values.astype(BF16)
        span = pl.ds(part * half, half)
        writes.append(pltpu.make_async_copy(ready.at[span], out.at[span, which], go.at[part]))
        writes[-1].start()
    for write in writes:
        write.wait()


def scale_rows(which, slots, scales, place, pieces, earlier):
    count, rows, width = pieces[0].shape
    count = 2 * count if len(pieces) == 8 else count
    operands = [scales, place, *pieces] + ([] if earlier is None else [earlier])
    return pl.pallas_call(
        lambda *refs: scale_kernel(which, slots, len(pieces), *refs),
        out_shape=jax.ShapeDtypeStruct((count, slots, rows, 4 * width), BF16),
        in_specs=[SMEM, SMEM] + anywhere(len(operands) - 2),
        out_specs=anywhere(1)[0],
        scratch_shapes=[
            pltpu.VMEM((8, count // 2, rows, width), BF16),
            pltpu.VMEM((count, rows, 4 * width), BF16),
            pltpu.SemaphoreType.DMA((8,)),
            pltpu.SemaphoreType.DMA((2,)),
        ],
        input_output_aliases={} if earlier is None else {len(operands) - 1: 0},
        compiler_params=params(0, 50),
        cost_estimate=cost(0, 48 * count * rows * width),
        name="scale",
    )(*operands)


def in_order(first, *later):
    return lax.optimization_barrier((first, *later))


def scatter_first(messages):
    return shift(messages[0], 1), shift(messages[1], -1)


def choose_second(messages, first, mine):
    _, _, keep_right, keep_left, own = messages
    half = own.shape[0] // 2
    from_left, from_right = first
    return jnp.where(mine, keep_right, from_left[half:]), jnp.where(mine, keep_left, from_right[half:])


def scatter_second(chosen):
    return shift(chosen[0], 1), shift(chosen[1], -1)


def merge(messages, first, second, away):
    own, half = messages[4], messages[4].shape[0] // 2
    low = jnp.where(away == 1, first[1][:half], second[0][:half])
    low = jnp.where(away == 0, own[:half], low)
    high = jnp.where(away == 3, first[0][:half], second[1][:half])
    high = jnp.where(away == 0, own[half : 2 * half], high)
    return jnp.concatenate([low, high], axis=0)


def gather_first(quarter):
    return quarter, shift(quarter, 1), shift(quarter, -1)


def gather_halves(low, high):
    left_low = shift(low, 1)
    right_high = shift(high, -1)
    left_high = shift(high, 1)
    right_low = shift(low, -1)
    far_low = shift(left_low, 1)
    far_high = shift(right_high, -1)
    return [low, left_low, right_low, far_low, high, left_high, right_high, far_high]


def gather_second(pieces):
    _, left, right = pieces
    half = left.shape[0] // 2
    return [*pieces, shift(left[:half], 1), shift(right[half:], -1)]


def per_device(
    gradients, stat_left, stat_right, inv_left, inv_right, owned_blocks, owner_counts, block_matrix
):
    dp_count = lax.axis_size("dp")
    owner_total = lax.axis_size("replica")
    dp_index = lax.axis_index("dp")
    me = lax.axis_index("replica")
    block_total, shard_rows, order = gradients.shape
    local_total = block_total // dp_count
    slot_total = inv_left.shape[2]
    width = order // owner_total
    half = dp_count // 2

    by_owner = gradients.reshape(dp_count, local_total, shard_rows, order)
    my_columns = lax.dynamic_slice(
        by_owner, (0, 0, 0, me * width), (dp_count, 1, shard_rows, width)
    ).reshape(dp_count, shard_rows, width)
    first_pieces = gather_first(over_dp(my_columns))
    second_block = over_dp(pick_block(by_owner, 1))
    blocks = [gather_second(first_pieces), [second_block]]

    slot_ids = jnp.arange(slot_total, dtype=jnp.int32)
    live = slot_ids[None, None, :] < owner_counts[:, :, None]
    replica_ids = jnp.arange(owner_total, dtype=jnp.int32)
    infos, owners = [], []
    for b in range(local_total):
        match = (owned_blocks == b) & live
        owners.append(jnp.sum(jnp.where(match, replica_ids[None, :, None], 0), axis=(1, 2)))
        slots = jnp.sum(jnp.where(match, slot_ids[None, None, :], 0), axis=(1, 2))
        owner = lax.dynamic_index_in_dim(owners[b], dp_index, 0, keepdims=False)
        slot = lax.dynamic_index_in_dim(slots, dp_index, 0, keepdims=False)
        away = lax.rem(owner - me + owner_total, owner_total)
        info = jnp.stack([slot, (away == 0).astype(jnp.int32), me, away])
        infos.append(info.astype(jnp.int32))

    away = [info[3] for info in infos]

    *sent, sums = apply_roots(infos[0], inv_left[0, 0], blocks[0], inv_right[0, 0])
    got = scatter_first(sent)
    sent_next = apply_roots(infos[1], inv_left[0, 0], blocks[1], inv_right[0, 0], sums)
    sent_next, got = in_order(sent_next, got)
    got_more = scatter_second(choose_second(sent, got, away[0] == 0))
    got_next = scatter_first(sent_next)
    first = over_dp(merge(sent, got, got_more, away[0]))

    chunk = lax.broadcasted_iota(jnp.int32, sent_next[2].shape, 0)
    lane = lax.broadcasted_iota(jnp.int32, sent_next[2].shape, 2)
    of_before = (chunk == half) & (lane < width // 2)
    mine = jnp.where(of_before, away[0], away[1]) == 0
    got_next_more = scatter_second(choose_second(sent_next, got_next, mine))
    far_off = jnp.where(of_before[half], away[0], away[1])
    sums = jnp.where(far_off == 1, got_next[1][2 * half], got_next_more[0][half])
    sums = jnp.where(far_off == 3, got_next[0][2 * half], sums)
    sums = jnp.where(far_off == 0, sent_next[4][2 * half], sums)
    sums = jnp.broadcast_to(sums[None, :EXTRA], (dp_count, EXTRA, width))
    quarter = merge(sent_next, got_next, got_next_more, away[1])
    second = over_dp(jnp.concatenate([quarter, sums], axis=1))

    pieces = gather_first(first)
    pieces, stat_left, stat_right = in_order(pieces, stat_left, stat_right)
    stats = update_stats(0, infos[0], blocks[0], stat_left, stat_right, None)
    gathered = gather_second(pieces)
    pieces_next = gather_halves(second[:half, :shard_rows], second[half:, :shard_rows])
    passed_on, stats = in_order((pieces_next[1], pieces_next[6]), stats)
    pieces_next[1], pieces_next[6] = passed_on
    stats = update_stats(1, infos[1], blocks[1], stat_left, stat_right, stats)
    sums = second[:, shard_rows : shard_rows + 6, :].astype(F32)
    sums = sums.reshape(dp_count, 2, 3, local_total, width // local_total)[..., 0]
    sums = jnp.sum(sums, axis=2) / SUM_SCALE
    sums = jnp.swapaxes(sums, 1, 2).reshape(block_total, 2)

    matrix_ids = jnp.arange(NMAT, dtype=jnp.int32)
    matrix_hot = (block_matrix[:, None] == matrix_ids[None, :]).astype(F32)
    totals = jnp.sum(matrix_hot[:, :, None] * sums[:, None, :], axis=0)
    graft = jnp.sqrt(totals[:, 1]) / jnp.sqrt(totals[:, 0] + EPSILON)
    scales = jnp.sum(matrix_hot * graft[None, :], axis=1)

    place = me.reshape(1).astype(jnp.int32)
    update = scale_rows(0, local_total, scales, place, gathered, None)
    update = scale_rows(1, local_total, scales, place, pieces_next, update)
    return (update.reshape(block_total, shard_rows, order), *stats)


def solution(mesh):
    return jax.shard_map(
        per_device,
        mesh=mesh,
        in_specs=(
            P(None, "dp", None),
            P("dp", "replica", None),
            P("dp", "replica", None),
            P("dp", "replica", None, None, None),
            P("dp", "replica", None, None, None),
            P(),
            P(),
            P(),
        ),
        out_specs=(P(None, "dp", None), P("dp", "replica", None), P("dp", "replica", None)),
        check_vma=False,
    )
```
